32 devices in a mesh: tm: 16 (over z, y, core), region: 2 (over x).
Axes of the slice: x: 2, y: 2, z: 4, core: 2. Of those that a mesh axis runs over, the one named last changes fastest.
Arguments:
- waveform: bfloat16 [192, 131072], P('region', 'tm'), may hold values from -220 to 220
- station_order: int32 [192], P('region'), may hold values from 0 to 191, each once
- library: float32 [128, 24, 200], P('tm'), may hold values from -6 to 6
- owner: int32 [4], replicated, may hold values from 0 to 15
- channels: int32 [4, 8, 24], replicated, may hold values from 0 to 191, as said below
Outputs:
- detection: float32 [4, 8, 131072], P(None, 'region', 'tm')
The draws below stay inside these ranges and needn't reach their ends.
Inputs may be any that keep to these rules, and one draw needn't show every extreme that they name: `channels`: within one template the 24 station channel ids differ.
All inputs are finite; a program needn't handle non-finite values.
Results may differ from the reference program's by a relative error of at most 0.003.
Values may be sent and summed in bfloat16 or wider, within the bound.
A program may use at most 64 MiB of HBM per device.

```python
import math
import jax
import jax.numpy as jnp
from jax import lax

CH = 192
TCH = 24
TAPS = 200
NTPL = 8
STEPS = 4
TIME = 131072
LIB = 128
N_TM = 16
N_REGION = 2


def draw_waveform(key, part):
    key_noise = jax.random.fold_in(key, 11)
    key_gain = jax.random.fold_in(key, 12)
    key_phase = jax.random.fold_in(key, 13)
    times = jnp.arange(TIME, dtype=jnp.int32)
    fraction = times.astype(jnp.float32)[None, :] / TIME
    channel_gain = jnp.exp(jax.random.uniform(key_gain, (CH, 1), jnp.float32, math.log(0.5), math.log(3.4)))
    starts = jax.random.randint(key_phase, (2,), 0, 4096, jnp.int32)
    period_one = TAPS // 5 + 1
    period_two = TAPS // 9 + 2
    angle_one = ((times + starts[0]) % period_one).astype(jnp.float32) * (2.0 * math.pi / period_one)
    angle_two = ((times + starts[1]) % period_two).astype(jnp.float32) * (2.0 * math.pi / period_two)
    shared = (jnp.sin(angle_one) + jnp.sin(angle_two))[None, :]
    random_part = jax.random.truncated_normal(key_noise, -3.0, 3.0, (CH, TIME), jnp.float32)
    envelope = jnp.exp(math.log(12.0) * fraction)
    values = channel_gain * envelope * (random_part + 0.8 * shared)
    return values.astype(jnp.bfloat16)


def draw_channels(key, part):
    row_keys = jax.random.split(jax.random.fold_in(key, 21), STEPS * NTPL)
    chosen = jax.vmap(lambda row_key: jax.random.permutation(row_key, CH)[:TCH])(row_keys).astype(jnp.int32)
    remainder = jax.random.permutation(jax.random.fold_in(key, 22), CH - 2)[:TCH - 2].astype(jnp.int32) + 1
    leading = jnp.concatenate([jnp.array([0, CH - 1], jnp.int32), remainder])
    chosen = chosen.at[0].set(leading)
    return chosen.reshape(STEPS, NTPL, TCH).astype(jnp.int32)


def touch_ends(entries, key, low, high):
    place = [jax.random.randint(jax.random.fold_in(key, axis), (), 0, length) for axis, length in enumerate(entries.shape)]
    longest = entries.shape.index(max(entries.shape))
    neighbour = place[:longest] + [(place[longest] + 1) % entries.shape[longest]] + place[longest + 1:]
    return entries.at[tuple(place)].set(low).at[tuple(neighbour)].set(high)


def block_scale(own_key, dims, shards, least, largest):
    loudness, own = 1.0, jax.random.fold_in(own_key, 6)
    for axis_at, blocks in shards:
        heights = jnp.exp(jax.random.uniform(jax.random.fold_in(own, axis_at), (blocks,), jnp.float32, least / len(shards), largest / len(shards)))
        loudness = loudness * jnp.repeat(heights, dims[axis_at] // blocks).reshape([-1 if axis == axis_at else 1 for axis in range(len(dims))])
    return loudness


def gaussian(rng, dims, scale, bound, shards=(), held_as=jnp.bfloat16):
    values = scale * jax.random.normal(rng, dims, jnp.float32)
    if shards:
        values = values * block_scale(rng, dims, shards, -0.22, 0.18)
    return jnp.clip(values, -bound, bound).astype(held_as)


def setup_inputs(seed: int = 0) -> dict:
    arg_keys = jax.random.split(jax.random.key(seed), 6)
    return {
        "waveform": draw_waveform(jax.random.fold_in(arg_keys[5], 71), 0),
        "station_order": jax.random.permutation(arg_keys[1], CH).astype(jnp.int32),
        "library": gaussian(arg_keys[2], (LIB, TCH, TAPS), 1.0, 6.0, ((0, 16),), jnp.float32),
        "owner": touch_ends(jax.random.randint(arg_keys[3], (STEPS,), 0, N_TM), jax.random.fold_in(arg_keys[3], 1), 0, N_TM - 1).astype(jnp.int32),
        "channels": draw_channels(jax.random.fold_in(arg_keys[5], 71), 0),
    }


water_level = 4.0
eps = 1e-06

def reference(waveform, station_order, library, owner, channels):
    padded = jnp.pad(waveform, ((0, 0), (0, TAPS - 1)))
    squares = padded.astype(jnp.float32) ** 2

    def add_square(tap_index, running):
        return running + lax.dynamic_slice_in_dim(squares, tap_index, TIME, 1)
    energy = lax.fori_loop(0, TAPS, add_square, jnp.zeros((CH, TIME), jnp.float32))
    inv_scale = 1.0 / jnp.sqrt(energy + TAPS * water_level)
    where_col = jnp.zeros((CH,), jnp.int32).at[station_order].set(jnp.arange(CH, dtype=jnp.int32))
    per_region = CH // N_REGION
    region_of = (where_col // per_region).astype(jnp.int32)
    region_onehot = (region_of[:, None] == jnp.arange(N_REGION, dtype=jnp.int32)[None, :]).astype(jnp.float32)
    outputs = []
    for step_index in range(STEPS):
        first_row = (owner[step_index] * NTPL).astype(jnp.int32)
        panel = lax.dynamic_slice_in_dim(library, first_row, NTPL, 0)
        centred = panel - lax.optimization_barrier(jnp.mean(panel, axis=2, keepdims=True))
        norm_taps = (centred / jnp.sqrt(lax.optimization_barrier(jnp.sum(centred * centred, axis=2, keepdims=True)) + eps)).astype(jnp.bfloat16)
        taps_wide = norm_taps.astype(jnp.float32)
        stations = channels[step_index]
        columns = where_col[stations]
        rows_data = padded[columns].astype(jnp.float32)

        def add_product(tap_index, running):
            weight = lax.dynamic_slice_in_dim(taps_wide, tap_index, 1, 2)
            return running + weight * lax.dynamic_slice_in_dim(rows_data, tap_index, TIME, 2)
        summed = lax.fori_loop(0, TAPS, add_product, jnp.zeros((NTPL, TCH, TIME), jnp.float32))
        correlation = summed * inv_scale[columns]
        partial_value = jnp.einsum('kjt,kjr->krt', correlation, region_onehot[columns], precision=lax.Precision.HIGHEST)
        stacked = lax.optimization_barrier(jnp.sum(partial_value, axis=1))
        mean_power = lax.optimization_barrier(jnp.sum(stacked * stacked, axis=1, keepdims=True)) / TIME + eps
        outputs.append(stacked / jnp.sqrt(mean_power))
    return jnp.stack(outputs)
```

```python
import functools
import jax
import jax.numpy as jnp
from jax import lax
from jax.experimental import pallas as pl
from jax.experimental.pallas import tpu as pltpu
from jax.sharding import PartitionSpec as P

water_level = 4.0
eps = 1e-06
offs = 32
depth = 256
rows_z = 288
unroll = 32
MESH = pl.DeviceIdType.MESH


def prepare_kernel(
    steps, count, owner_ref, library_ref, x_ref, edge_ref, z_ref, inv_ref, taps_ref,
    mine, got, sel, full, halo, halo_f, ext, halo_sems, one_send, one_recv, two_send, two_recv,
):
    me = lax.axis_index("tm")
    region = lax.axis_index("region")
    barrier = pltpu.get_barrier_semaphore()
    for d in range(1, count):
        pl.semaphore_signal(barrier, inc=1, device_id=(lax.rem(me + d, count), region), device_id_type=MESH)

    taps = library_ref.shape[1]
    tiles = mine.shape[0]
    panel = library_ref[...]
    centred = panel - jnp.sum(panel, axis=1, keepdims=True) / taps
    normed = centred / jnp.sqrt(jnp.sum(centred * centred, axis=1, keepdims=True) + eps)
    normed = jnp.concatenate([normed, jnp.zeros((panel.shape[0], depth - taps), jnp.float32)], axis=1)
    mine[...] = normed.astype(jnp.bfloat16).reshape(tiles, 16, depth)

    holders = [u * count // tiles for u in range(tiles)]
    my_tile = (me * tiles + count - 1) // count
    holding = my_tile * count // tiles == me
    my_tile = jnp.minimum(my_tile, tiles - 1)

    pl.semaphore_wait(barrier, count - 1)
    left = lax.rem(me + count - 1, count)
    edge_copy = pltpu.make_async_remote_copy(
        src_ref=edge_ref, dst_ref=halo, send_sem=halo_sems.at[0], recv_sem=halo_sems.at[1],
        device_id=(left, region), device_id_type=MESH,
    )
    edge_copy.start()

    def piece(u):
        return pltpu.make_async_remote_copy(
            src_ref=mine.at[u], dst_ref=got.at[me], send_sem=one_send.at[u], recv_sem=one_recv.at[me],
            device_id=(holders[u], region), device_id_type=MESH,
        )

    for u in range(tiles):
        @pl.when(me != holders[u])
        def _():
            piece(u).start()

    chans, blocks, _ = x_ref.shape
    lane = lax.broadcasted_iota(jnp.int32, (1, 128), 1)
    low_half = lane < 64
    spread = lax.broadcasted_iota(jnp.int32, (offs, depth), 1) - lax.broadcasted_iota(jnp.int32, (offs, depth), 0)
    band = ((spread >= 0) & (spread < taps)).astype(jnp.float32).astype(jnp.bfloat16)
    width = ext.shape[0]

    def channel(c, slot):
        ext[slot, 0:blocks] = x_ref[c].astype(jnp.float32)
        rim = halo_f[pl.ds(c, 1), :]
        ext[slot, blocks : blocks + 1] = rim[:, 0:128]
        ext[slot, blocks + 1 : blocks + 2] = rim[:, 128:256]
        x = [ext[slot, m : m + blocks] for m in range(3)]
        y = [pltpu.roll(v, 64, 1) for v in x]
        columns = []
        for m in range(3):
            second = jnp.where(low_half, y[m], y[m + 1]) if m < 2 else y[m]
            columns.append(jnp.concatenate([x[m], second], axis=0).T)
        z = jnp.concatenate([columns[0], columns[1], columns[2][: rows_z - 256]], axis=0)
        z_ref[c] = z.astype(jnp.bfloat16)
        square = z * z
        high = square.astype(jnp.bfloat16)
        low = (square - high.astype(jnp.float32)).astype(jnp.bfloat16)

        def both(v):
            return jnp.concatenate([v[0:depth], v[offs : offs + depth]], axis=1)

        energy = jnp.dot(band, both(high), preferred_element_type=jnp.float32)
        energy = energy + jnp.dot(band, both(low), preferred_element_type=jnp.float32)
        inv_ref[c] = lax.rsqrt(energy + taps * water_level)

    def windows(first, last):
        def group(i, carry):
            for slot in range(width):
                channel(i * width + slot, slot)
            return carry

        lax.fori_loop(first // width, last // width, group, 0)

    edge_copy.wait()
    inside = (me < count - 1) & (lax.broadcasted_iota(jnp.int32, (chans, depth), 1) < taps - 1)
    halo_f[...] = jnp.where(inside, halo[...].astype(jnp.float32), 0.0)
    split = chans // 3 // width * width
    windows(0, split)

    for u in range(tiles):
        @pl.when(me != holders[u])
        def _():
            piece(u).wait_send()

    def spread_copy(d):
        return pltpu.make_async_remote_copy(
            src_ref=sel, dst_ref=full.at[my_tile], send_sem=two_send.at[d - 1], recv_sem=two_recv.at[my_tile],
            device_id=(lax.rem(me + d, count), region), device_id_type=MESH,
        )

    @pl.when(holding)
    def _():
        for i in range(count):
            @pl.when(me != i)
            def _():
                pltpu.make_async_remote_copy(
                    src_ref=mine.at[0], dst_ref=got.at[i], send_sem=one_send.at[0], recv_sem=one_recv.at[i],
                    device_id=(left, region), device_id_type=MESH,
                ).wait_recv()
        got[me] = mine[my_tile]
        for s in range(steps):
            sel[s] = got[owner_ref[s]]
        full[my_tile] = sel[...]
        for d in range(1, count):
            spread_copy(d).start()

    windows(split, chans)

    for u in range(tiles):
        @pl.when(me != holders[u])
        def _():
            pltpu.make_async_remote_copy(
                src_ref=sel, dst_ref=full.at[u], send_sem=two_send.at[0], recv_sem=two_recv.at[u],
                device_id=(left, region), device_id_type=MESH,
            ).wait_recv()

    taps_ref[0 : tiles * steps * 16] = full[...].astype(jnp.float32).reshape(tiles * steps * 16, depth)
    taps_ref[tiles * steps * 16 :] = jnp.zeros((8, depth), jnp.float32)

    @pl.when(holding)
    def _():
        for d in range(1, count):
            spread_copy(d).wait_send()


def pair_kernel(code_ref, z_ref, inv_ref, taps_ref, out_ref, acc_ref, list_ref):
    templates = out_ref.shape[0]

    def compact(i, filled):
        code = code_ref[i]
        list_ref[filled] = code
        return filled + jnp.where(code >= 0, 1, 0)

    count = lax.fori_loop(0, code_ref.shape[0], compact, 0, unroll=8)
    for u in range(unroll):
        list_ref[count + u] = templates
    acc_ref[...] = jnp.zeros_like(acc_ref)

    def one_pair(code):
        template = code & 63
        col = (code >> 6) & 255
        row = code >> 14
        base = jnp.broadcast_to(taps_ref[pl.ds(row, 1)], (8, depth))
        base = pltpu.roll(base, 0, 1, stride=1, stride_axis=0)
        shifted = [base] + [pltpu.roll(base, a, 1) for a in range(8, offs, 8)]
        matrix = jnp.concatenate(shifted, axis=0).astype(jnp.bfloat16)
        window = jnp.concatenate([z_ref[col, 0:depth], z_ref[col, offs : offs + depth]], axis=1)
        product = jnp.dot(matrix, window, preferred_element_type=jnp.float32)
        return template, product * inv_ref[col]

    def group(i, carry):
        done = [one_pair(list_ref[i * unroll + u]) for u in range(unroll)]
        for template, value in done:
            acc_ref[template] += value
        return carry

    lax.fori_loop(0, (count + unroll - 1) // unroll, group, 0)
    out_ref[...] = acc_ref[:templates]


def finish_kernel(total_time, steps, count, regions, parts_ref, out_ref, sent, arrived, stacked, power_sent, power_got, x_send, x_recv, p_send, p_recv):
    me = lax.axis_index("tm")
    region = lax.axis_index("region")
    barrier = pltpu.get_barrier_semaphore()
    for d in range(1, regions):
        pl.semaphore_signal(barrier, inc=1, device_id=(me, lax.rem(region + d, regions)), device_id_type=MESH)
    for d in range(1, count):
        pl.semaphore_signal(barrier, inc=1, device_id=(lax.rem(me + d, count), region), device_id_type=MESH)
    held = out_ref.shape[0]
    per = held // steps

    def chunk(d, s):
        return pltpu.make_async_remote_copy(
            src_ref=sent.at[d - 1, s], dst_ref=arrived.at[d - 1, s], send_sem=x_send.at[d - 1, s], recv_sem=x_recv.at[d - 1, s],
            device_id=(me, lax.rem(region + d, regions)), device_id_type=MESH,
        )

    for s in range(steps):
        for d in range(1, regions):
            other = lax.rem(region + d, regions)
            sent[d - 1, s] = parts_ref[pl.ds(other * held + s * per, per)].astype(jnp.bfloat16)
        if s == 0:
            pl.semaphore_wait(barrier, count - 1 + regions - 1)
        for d in range(1, regions):
            chunk(d, s).start()
    lane = lax.broadcasted_iota(jnp.int32, (1, 128), 1)
    power = jnp.zeros((1, 128), jnp.float32)
    for s in range(steps):
        for d in range(1, regions):
            chunk(d, s).wait_recv()
        for k in range(per):
            at = s * per + k
            value = parts_ref[region * held + at]
            for d in range(1, regions):
                value = value + arrived[d - 1, s, k].astype(jnp.float32)
            total = jnp.sum(jnp.sum(value * value, axis=0, keepdims=True), axis=1, keepdims=True)
            power = power + jnp.where(lane == at, total, 0.0)
            upright = jnp.concatenate([value[:, :128], value[:, 128:]], axis=0).T
            stacked[at] = jnp.concatenate([upright[:64], upright[64:]], axis=1)
    power_sent[...] = power
    copies = []
    for d in range(1, count):
        copy = pltpu.make_async_remote_copy(
            src_ref=power_sent, dst_ref=power_got.at[d - 1], send_sem=p_send.at[d - 1], recv_sem=p_recv.at[d - 1],
            device_id=(lax.rem(me + d, count), region), device_id_type=MESH,
        )
        copy.start()
        copies.append(copy)
    for copy in copies:
        copy.wait_recv()
    power = power + jnp.sum(power_got[...], axis=0)
    factor = lax.rsqrt(power / total_time + eps)
    for at in range(held):
        one = jnp.sum(jnp.where(lane == at, factor, 0.0), axis=1, keepdims=True)
        out_ref[at] = stacked[at] * one
    for s in range(steps):
        for d in range(1, regions):
            chunk(d, s).wait_send()
    for copy in copies:
        copy.wait_send()


def pair_list(station_order, channels, regions):
    steps, templates, used = channels.shape
    per = templates // regions
    match = (channels.reshape(-1)[:, None] == station_order[None, :]).astype(jnp.int32)
    local = jnp.sum(match, axis=1)
    col = jnp.sum(match * jnp.arange(station_order.shape[0], dtype=jnp.int32)[None, :], axis=1)
    pair = jnp.arange(steps * templates * used, dtype=jnp.int32)
    step = pair // (templates * used)
    inner = pair % (templates * used)
    row = (inner // 16 * steps + step) * 16 + inner % 16
    k = inner // used
    template = (k // per) * (steps * per) + step * per + k % per
    code = (row << 14) | (col << 6) | template
    return jnp.where(local > 0, code, -1)


def body(waveform, station_order, library, owner, channels):
    chans, time_local = waveform.shape
    blocks = time_local // 128
    steps, templates, used = channels.shape
    tap_count = library.shape[2]
    count = lax.axis_size("tm")
    regions = lax.axis_size("region")
    per = templates // regions
    held = steps * per
    all_templates = steps * templates
    pairs = all_templates * used
    tiles = templates * used // 16
    lanes = time_local // offs
    wide = 4

    vmem = pl.BlockSpec(memory_space=pltpu.VMEM)
    smem = pl.BlockSpec(memory_space=pltpu.SMEM)
    dma = pltpu.SemaphoreType.DMA
    z, inv_scale, taps = pl.pallas_call(
        functools.partial(prepare_kernel, steps, count),
        out_shape=[
            jax.ShapeDtypeStruct((chans, rows_z, 128), jnp.bfloat16),
            jax.ShapeDtypeStruct((chans, offs, lanes), jnp.float32),
            jax.ShapeDtypeStruct((pairs + 8, depth), jnp.float32),
        ],
        in_specs=[smem, vmem, vmem, vmem],
        out_specs=[vmem, vmem, vmem],
        scratch_shapes=[
            pltpu.VMEM((tiles, 16, depth), jnp.bfloat16),
            pltpu.VMEM((count, 16, depth), jnp.bfloat16),
            pltpu.VMEM((steps, 16, depth), jnp.bfloat16),
            pltpu.VMEM((tiles, steps, 16, depth), jnp.bfloat16),
            pltpu.VMEM((chans, depth), jnp.bfloat16),
            pltpu.VMEM((chans, depth), jnp.float32),
            pltpu.VMEM((wide, blocks + 8, 128), jnp.float32),
            dma((2,)),
            dma((tiles,)),
            dma((count,)),
            dma((count - 1,)),
            dma((tiles,)),
        ],
        compiler_params=pltpu.CompilerParams(collective_id=0, has_side_effects=True, vmem_limit_bytes=40 * 2**20),
        name="prepare",
    )(owner, library.reshape(templates * used, tap_count), waveform.reshape(chans, blocks, 128), waveform[:, :depth])

    codes = pair_list(station_order, channels, regions)
    parts = pl.pallas_call(
        pair_kernel,
        out_shape=jax.ShapeDtypeStruct((all_templates, offs, lanes), jnp.float32),
        in_specs=[smem, vmem, vmem, vmem],
        out_specs=vmem,
        scratch_shapes=[
            pltpu.VMEM((all_templates + 1, offs, lanes), jnp.float32),
            pltpu.SMEM((pairs + unroll,), jnp.int32),
        ],
        compiler_params=pltpu.CompilerParams(vmem_limit_bytes=40 * 2**20),
        name="pairs",
    )(codes, z, inv_scale, taps)

    result = pl.pallas_call(
        functools.partial(finish_kernel, time_local * count, steps, count, regions),
        out_shape=jax.ShapeDtypeStruct((held, blocks, 128), jnp.float32),
        in_specs=[vmem],
        out_specs=vmem,
        scratch_shapes=[
            pltpu.VMEM((regions - 1, steps, per, offs, lanes), jnp.bfloat16),
            pltpu.VMEM((regions - 1, steps, per, offs, lanes), jnp.bfloat16),
            pltpu.VMEM((held, blocks, 128), jnp.float32),
            pltpu.VMEM((1, 128), jnp.float32),
            pltpu.VMEM((count - 1, 1, 128), jnp.float32),
            dma((regions - 1, steps)),
            dma((regions - 1, steps)),
            dma((count - 1,)),
            dma((count - 1,)),
        ],
        compiler_params=pltpu.CompilerParams(collective_id=1, has_side_effects=True, vmem_limit_bytes=40 * 2**20),
        name="finish",
    )(parts)
    return result.reshape(steps, per, time_local)


def solution(mesh):
    in_specs = (P("region", "tm"), P("region"), P("tm", None, None), P(), P())
    out_specs = P(None, "region", "tm")
    return jax.shard_map(body, mesh=mesh, in_specs=in_specs, out_specs=out_specs, check_vma=False)
```

```python
import functools
import jax
import jax.numpy as jnp
from jax import lax
from jax.experimental import pallas as pl
from jax.experimental.pallas import tpu as pltpu
from jax.sharding import PartitionSpec as P

water_level = 4.0
eps = 1e-06
offs = 32
depth = 256
rows_z = 288
unroll = 16
MESH = pl.DeviceIdType.MESH


def pair_lists(steps, regions, region, order_ref, channels_ref, list_ref):
    rows, used = channels_ref.shape
    templates = rows // steps
    per = templates // regions
    held = steps * per
    chans = order_ref.shape[1]
    length = list_ref.shape[2]
    f32, bf16 = jnp.float32, jnp.bfloat16
    order = order_ref[...]
    table = channels_ref[...]
    hit = jnp.zeros((rows, chans), jnp.int32)
    place = jnp.zeros((rows, chans), jnp.int32)
    for j in range(used):
        same = jnp.broadcast_to(table[:, j : j + 1], (rows, chans)) == order
        hit = hit + jnp.where(same, 1, 0)
        place = place + jnp.where(same, j, 0)
    one = lax.broadcasted_iota(jnp.int32, (rows, rows), 0)
    two = lax.broadcasted_iota(jnp.int32, (rows, rows), 1)
    together = one % templates // per == two % templates // per

    def ones(mask):
        return jnp.where(mask, 1.0, 0.0).astype(bf16)

    hits = hit.astype(f32)
    rank = jnp.dot(ones(together & (two < one)), hits.astype(bf16), preferred_element_type=f32)
    amount = jnp.dot(ones(together), hits.astype(bf16), preferred_element_type=f32)
    entries = jnp.floor((amount + 1) * 0.5)
    before = ones(lax.broadcasted_iota(jnp.int32, (chans, chans), 0) < lax.broadcasted_iota(jnp.int32, (chans, chans), 1))
    first = jnp.dot(entries.astype(bf16), before, preferred_element_type=f32)
    position = jnp.where(hits > 0, 2 * first + rank, -1.0)
    row = lax.broadcasted_iota(jnp.int32, (rows, chans), 0)
    step = row // templates
    inner = row % templates * used + place
    source = (inner // 16 * steps + step) * 16 + inner % 16
    target = step * per + row % templates % per
    column = lax.broadcasted_iota(jnp.int32, (rows, chans), 1)
    empty = held * 2**17 + rows * used
    code = (target * 2**17 + column * 2**10 + source - empty).astype(f32)
    blank = jnp.zeros((rows, 128 - chans), f32)
    position = jnp.concatenate([position, blank - 1], axis=1).T
    code = jnp.concatenate([code, blank], axis=1).T
    total = jnp.sum(entries, axis=1, keepdims=True)
    for g in range(regions):
        mine = [s * templates + g * per + k for s in range(steps) for k in range(per)]
        for base in range(0, length, 128):
            index = (lax.broadcasted_iota(jnp.int32, (128, 128), 1) + base).astype(f32)
            found = jnp.zeros((128, 128), f32)
            for t in mine:
                found = found + jnp.where(position[:, t : t + 1] == index, code[:, t : t + 1], 0.0)
            line = jnp.sum(found, axis=0, keepdims=True).astype(jnp.int32) + empty
            if base + 128 == length:
                last = lax.broadcasted_iota(jnp.int32, (1, 128), 1) == 127
                line = jnp.where(last, total[mine[0] : mine[0] + 1].astype(jnp.int32), line)
            list_ref[lax.rem(g - region - 1 + 2 * regions, regions), 0:1, base : base + 128] = line


def prepare_kernel(
    steps, count, regions, owner_ref, library_ref, x_ref, edge_ref, order_ref, channels_ref, z_ref, inv_ref, taps_ref, list_ref,
    mine, got, sel, full, halo, halo_f, ext, halo_sems, one_send, one_recv, two_send, two_recv,
):
    me = lax.axis_index("tm")
    region = lax.axis_index("region")
    barrier = pltpu.get_barrier_semaphore()
    for d in range(1, count):
        pl.semaphore_signal(barrier, inc=1, device_id=(lax.rem(me + d, count), region), device_id_type=MESH)

    taps = library_ref.shape[1]
    tiles = mine.shape[0]
    panel = library_ref[...]
    centred = panel - jnp.sum(panel, axis=1, keepdims=True) / taps
    normed = centred / jnp.sqrt(jnp.sum(centred * centred, axis=1, keepdims=True) + eps)
    normed = jnp.concatenate([normed, jnp.zeros((panel.shape[0], depth - taps), jnp.float32)], axis=1)
    mine[...] = normed.astype(jnp.bfloat16).reshape(tiles, 16, depth)

    holders = [u * count // tiles for u in range(tiles)]
    my_tile = (me * tiles + count - 1) // count
    holding = my_tile * count // tiles == me
    my_tile = jnp.minimum(my_tile, tiles - 1)

    pl.semaphore_wait(barrier, count - 1)
    left = lax.rem(me + count - 1, count)
    edge_copy = pltpu.make_async_remote_copy(
        src_ref=edge_ref, dst_ref=halo, send_sem=halo_sems.at[0], recv_sem=halo_sems.at[1],
        device_id=(left, region), device_id_type=MESH,
    )
    edge_copy.start()

    def piece(u):
        return pltpu.make_async_remote_copy(
            src_ref=mine.at[u], dst_ref=got.at[me], send_sem=one_send.at[u], recv_sem=one_recv.at[me],
            device_id=(holders[u], region), device_id_type=MESH,
        )

    for u in range(tiles):
        @pl.when(me != holders[u])
        def _():
            piece(u).start()

    chans, blocks, _ = x_ref.shape
    lane = lax.broadcasted_iota(jnp.int32, (1, 128), 1)
    low_half = lane < 64
    spread = lax.broadcasted_iota(jnp.int32, (offs, depth), 1) - lax.broadcasted_iota(jnp.int32, (offs, depth), 0)
    band = ((spread >= 0) & (spread < taps)).astype(jnp.float32).astype(jnp.bfloat16)
    width = ext.shape[0]

    def channel(c, slot):
        ext[slot, 0:blocks] = x_ref[c].astype(jnp.float32)
        rim = halo_f[pl.ds(c, 1), :]
        ext[slot, blocks : blocks + 1] = rim[:, 0:128]
        ext[slot, blocks + 1 : blocks + 2] = rim[:, 128:256]
        x = [ext[slot, m : m + blocks] for m in range(3)]
        y = [pltpu.roll(v, 64, 1) for v in x]
        columns = []
        for m in range(3):
            second = jnp.where(low_half, y[m], y[m + 1]) if m < 2 else y[m]
            columns.append(jnp.concatenate([x[m], second], axis=0).T)
        z = jnp.concatenate([columns[0], columns[1], columns[2][: rows_z - 256]], axis=0)
        z_ref[c] = z.astype(jnp.bfloat16)
        square = z * z
        high = square.astype(jnp.bfloat16)
        low = (square - high.astype(jnp.float32)).astype(jnp.bfloat16)

        def both(v):
            return jnp.concatenate([v[0:depth], v[offs : offs + depth]], axis=1)

        energy = jnp.dot(band, both(high), preferred_element_type=jnp.float32)
        energy = energy + jnp.dot(band, both(low), preferred_element_type=jnp.float32)
        inv_ref[c] = lax.rsqrt(energy + taps * water_level)

    def windows(first, last):
        def group(i, carry):
            for slot in range(width):
                channel(i * width + slot, slot)
            return carry

        lax.fori_loop(first // width, last // width, group, 0)

    pair_lists(steps, regions, region, order_ref, channels_ref, list_ref)

    edge_copy.wait()
    inside = (me < count - 1) & (lax.broadcasted_iota(jnp.int32, (chans, depth), 1) < taps - 1)
    halo_f[...] = jnp.where(inside, halo[...].astype(jnp.float32), 0.0)

    for u in range(tiles):
        @pl.when(me != holders[u])
        def _():
            piece(u).wait_send()

    def spread_copy(d):
        return pltpu.make_async_remote_copy(
            src_ref=sel, dst_ref=full.at[my_tile], send_sem=two_send.at[d - 1], recv_sem=two_recv.at[my_tile],
            device_id=(lax.rem(me + d, count), region), device_id_type=MESH,
        )

    @pl.when(holding)
    def _():
        for i in range(count):
            @pl.when(me != i)
            def _():
                pltpu.make_async_remote_copy(
                    src_ref=mine.at[0], dst_ref=got.at[i], send_sem=one_send.at[0], recv_sem=one_recv.at[i],
                    device_id=(left, region), device_id_type=MESH,
                ).wait_recv()
        got[me] = mine[my_tile]
        for s in range(steps):
            sel[s] = got[owner_ref[s]]
        full[my_tile] = sel[...]
        for d in range(1, count):
            spread_copy(d).start()

    windows(0, chans)

    for u in range(tiles):
        @pl.when(me != holders[u])
        def _():
            pltpu.make_async_remote_copy(
                src_ref=sel, dst_ref=full.at[u], send_sem=two_send.at[0], recv_sem=two_recv.at[u],
                device_id=(left, region), device_id_type=MESH,
            ).wait_recv()

    taps_ref[0 : tiles * steps * 16] = full[...].astype(jnp.float32).reshape(tiles * steps * 16, depth)
    taps_ref[tiles * steps * 16 :] = jnp.zeros((8, depth), jnp.float32)

    @pl.when(holding)
    def _():
        for d in range(1, count):
            spread_copy(d).wait_send()


def pair_kernel(which, list_ref, z_ref, inv_ref, taps_ref, out_ref, acc_ref):
    held = out_ref.shape[0]
    total = list_ref[which, 0, list_ref.shape[2] - 1]
    acc_ref[...] = jnp.zeros_like(acc_ref)

    def shifted(row):
        base = jnp.broadcast_to(taps_ref[pl.ds(row, 1)], (8, depth))
        base = pltpu.roll(base, 0, 1, stride=1, stride_axis=0)
        return [base] + [pltpu.roll(base, a, 1) for a in range(8, offs, 8)]

    def entry(e):
        codes = [list_ref[which, 0, 2 * e + i] for i in range(2)]
        matrix = jnp.concatenate(shifted(codes[0] & 1023) + shifted(codes[1] & 1023), axis=0).astype(jnp.bfloat16)
        col = (codes[0] >> 10) & 127
        window = jnp.concatenate([z_ref[col, 0:depth], z_ref[col, offs : offs + depth]], axis=1)
        product = jnp.dot(matrix, window, preferred_element_type=jnp.float32)
        scale = inv_ref[col]
        return [(codes[i] >> 17, product[i * offs : (i + 1) * offs] * scale) for i in range(2)]

    def group(i, carry):
        done = [entry(i * unroll + u) for u in range(unroll)]
        for both in done:
            for template, value in both:
                acc_ref[template] += value
        return carry

    lax.fori_loop(0, (total + unroll - 1) // unroll, group, 0)
    out_ref[...] = acc_ref[:held].astype(out_ref.dtype)


def finish_kernel(total_time, count, *refs):
    *parts, out_ref, stacked, power_sent, power_got, p_send, p_recv = refs
    me = lax.axis_index("tm")
    region = lax.axis_index("region")
    barrier = pltpu.get_barrier_semaphore()
    for d in range(1, count):
        pl.semaphore_signal(barrier, inc=1, device_id=(lax.rem(me + d, count), region), device_id_type=MESH)
    held = out_ref.shape[0]
    lane = lax.broadcasted_iota(jnp.int32, (1, 128), 1)
    power = jnp.zeros((1, 128), jnp.float32)
    for at in range(held):
        value = parts[-1][at]
        for other in parts[:-1]:
            value = value + other[at].astype(jnp.float32)
        total = jnp.sum(jnp.sum(value * value, axis=0, keepdims=True), axis=1, keepdims=True)
        power = power + jnp.where(lane == at, total, 0.0)
        upright = jnp.concatenate([value[:, :128], value[:, 128:]], axis=0).T
        stacked[at] = jnp.concatenate([upright[:64], upright[64:]], axis=1)
    power_sent[...] = power
    pl.semaphore_wait(barrier, count - 1)
    copies = []
    for d in range(1, count):
        copy = pltpu.make_async_remote_copy(
            src_ref=power_sent, dst_ref=power_got.at[d - 1], send_sem=p_send.at[d - 1], recv_sem=p_recv.at[d - 1],
            device_id=(lax.rem(me + d, count), region), device_id_type=MESH,
        )
        copy.start()
        copies.append(copy)
    for copy in copies:
        copy.wait()
    power = power + jnp.sum(power_got[...], axis=0)
    factor = lax.rsqrt(power / total_time + eps)
    for at in range(held):
        one = jnp.sum(jnp.where(lane == at, factor, 0.0), axis=1, keepdims=True)
        out_ref[at] = stacked[at] * one


def body(waveform, station_order, library, owner, channels):
    chans, time_local = waveform.shape
    blocks = time_local // 128
    steps, templates, used = channels.shape
    tap_count = library.shape[2]
    count = lax.axis_size("tm")
    regions = lax.axis_size("region")
    per = templates // regions
    held = steps * per
    all_templates = steps * templates
    pairs = all_templates * used
    tiles = templates * used // 16
    lanes = time_local // offs
    wide = 8

    vmem = pl.BlockSpec(memory_space=pltpu.VMEM)
    smem = pl.BlockSpec(memory_space=pltpu.SMEM)
    dma = pltpu.SemaphoreType.DMA
    length = -(-(held * used + chans + 2 * unroll + 1) // 128) * 128
    z, inv_scale, taps, lists = pl.pallas_call(
        functools.partial(prepare_kernel, steps, count, regions),
        out_shape=[
            jax.ShapeDtypeStruct((chans, rows_z, 128), jnp.bfloat16),
            jax.ShapeDtypeStruct((chans, offs, lanes), jnp.float32),
            jax.ShapeDtypeStruct((pairs + 8, depth), jnp.float32),
            jax.ShapeDtypeStruct((regions, 1, length), jnp.int32),
        ],
        in_specs=[smem] + [vmem] * 5,
        out_specs=[vmem] * 4,
        scratch_shapes=[
            pltpu.VMEM((tiles, 16, depth), jnp.bfloat16),
            pltpu.VMEM((count, 16, depth), jnp.bfloat16),
            pltpu.VMEM((steps, 16, depth), jnp.bfloat16),
            pltpu.VMEM((tiles, steps, 16, depth), jnp.bfloat16),
            pltpu.VMEM((chans, depth), jnp.bfloat16),
            pltpu.VMEM((chans, depth), jnp.float32),
            pltpu.VMEM((wide, blocks + 8, 128), jnp.float32),
            dma((2,)),
            dma((tiles,)),
            dma((count,)),
            dma((count - 1,)),
            dma((tiles,)),
        ],
        compiler_params=pltpu.CompilerParams(collective_id=0, has_side_effects=True, vmem_limit_bytes=16 * 2**20),
        name="prepare",
    )(
        owner, library.reshape(templates * used, tap_count), waveform.reshape(chans, blocks, 128), waveform[:, :depth],
        station_order.reshape(1, chans), channels.reshape(all_templates, used),
    )

    def partial_sums(which, dtype):
        return pl.pallas_call(
            functools.partial(pair_kernel, which),
            out_shape=jax.ShapeDtypeStruct((held, offs, lanes), dtype),
            in_specs=[smem, vmem, vmem, vmem],
            out_specs=vmem,
            scratch_shapes=[pltpu.VMEM((held + 1, offs, lanes), jnp.float32)],
            compiler_params=pltpu.CompilerParams(vmem_limit_bytes=16 * 2**20),
            cost_estimate=pl.CostEstimate(flops=held * used * offs * depth * lanes, bytes_accessed=12 * 2**20, transcendentals=0),
            name="pairs",
        )(lists, z, inv_scale, taps)

    parts = []
    for d in range(1, regions):
        part = partial_sums(d - 1, jnp.bfloat16)
        parts.append(lax.ppermute(part, "region", [(i, (i + d) % regions) for i in range(regions)]))
    parts.append(partial_sums(regions - 1, jnp.float32))

    result = pl.pallas_call(
        functools.partial(finish_kernel, time_local * count, count),
        out_shape=jax.ShapeDtypeStruct((held, blocks, 128), jnp.float32),
        in_specs=[vmem] * regions,
        out_specs=vmem,
        scratch_shapes=[
            pltpu.VMEM((held, blocks, 128), jnp.float32),
            pltpu.VMEM((1, 128), jnp.float32),
            pltpu.VMEM((count - 1, 1, 128), jnp.float32),
            dma((count - 1,)),
            dma((count - 1,)),
        ],
        compiler_params=pltpu.CompilerParams(collective_id=1, has_side_effects=True, vmem_limit_bytes=16 * 2**20),
        name="finish",
    )(*parts)
    return result.reshape(steps, per, time_local)


def solution(mesh):
    in_specs = (P("region", "tm"), P("region"), P("tm", None, None), P(), P())
    out_specs = P(None, "region", "tm")
    return jax.shard_map(body, mesh=mesh, in_specs=in_specs, out_specs=out_specs, check_vma=False)
```

```python
import functools
import jax
import jax.numpy as jnp
from jax import lax
from jax.experimental import pallas as pl
from jax.experimental.pallas import tpu as pltpu
from jax.sharding import PartitionSpec as P

water_level = 4.0
eps = 1e-06
offs = 32
depth = 256
rows_z = 288
unroll = 32
MESH = pl.DeviceIdType.MESH


def pair_lists(steps, regions, region, order_ref, channels_ref, list_ref):
    rows, used = channels_ref.shape
    templates = rows // steps
    per = templates // regions
    held = steps * per
    chans = order_ref.shape[1]
    length = list_ref.shape[2]
    f32, bf16 = jnp.float32, jnp.bfloat16
    order = order_ref[...]
    table = channels_ref[...]
    hit = jnp.zeros((rows, chans), jnp.int32)
    place = jnp.zeros((rows, chans), jnp.int32)
    for j in range(used):
        same = jnp.broadcast_to(table[:, j : j + 1], (rows, chans)) == order
        hit = hit + jnp.where(same, 1, 0)
        place = place + jnp.where(same, j, 0)
    one = lax.broadcasted_iota(jnp.int32, (rows, rows), 0)
    two = lax.broadcasted_iota(jnp.int32, (rows, rows), 1)
    together = one % templates // per == two % templates // per

    def ones(mask):
        return jnp.where(mask, 1.0, 0.0).astype(bf16)

    hits = hit.astype(f32)
    rank = jnp.dot(ones(together & (two < one)), hits.astype(bf16), preferred_element_type=f32)
    amount = jnp.dot(ones(together), hits.astype(bf16), preferred_element_type=f32)
    entries = jnp.floor((amount + 1) * 0.5)
    before = ones(lax.broadcasted_iota(jnp.int32, (chans, chans), 0) < lax.broadcasted_iota(jnp.int32, (chans, chans), 1))
    first = jnp.dot(entries.astype(bf16), before, preferred_element_type=f32)
    position = jnp.where(hits > 0, 2 * first + rank, -1.0)
    row = lax.broadcasted_iota(jnp.int32, (rows, chans), 0)
    step = row // templates
    inner = row % templates * used + place
    source = (inner // 16 * steps + step) * 16 + inner % 16
    target = step * per + row % templates % per
    column = lax.broadcasted_iota(jnp.int32, (rows, chans), 1)
    empty = held * 2**17 + rows * used
    code = (target * 2**17 + column * 2**10 + source - empty).astype(f32)
    blank = jnp.zeros((rows, 128 - chans), f32)
    position = jnp.concatenate([position, blank - 1], axis=1).T
    code = jnp.concatenate([code, blank], axis=1).T
    total = jnp.sum(entries, axis=1, keepdims=True)
    for g in range(regions):
        mine = [s * templates + g * per + k for s in range(steps) for k in range(per)]
        for base in range(0, length, 128):
            index = (lax.broadcasted_iota(jnp.int32, (128, 128), 1) + base).astype(f32)
            found = jnp.zeros((128, 128), f32)
            for t in mine:
                found = found + jnp.where(position[:, t : t + 1] == index, code[:, t : t + 1], 0.0)
            line = jnp.sum(found, axis=0, keepdims=True).astype(jnp.int32) + empty
            if base + 128 == length:
                last = lax.broadcasted_iota(jnp.int32, (1, 128), 1) == 127
                line = jnp.where(last, total[mine[0] : mine[0] + 1].astype(jnp.int32), line)
            list_ref[lax.rem(g - region - 1 + 2 * regions, regions), 0:1, base : base + 128] = line


def prepare_kernel(
    steps, count, regions, owner_hbm, library_hbm, x_ref, order_hbm, channels_hbm, z_ref, inv_ref, taps_ref, list_ref,
    owner_ref, library_ref, order_ref, channels_ref, small_sems, mine, got, sel, full, halo, local, ext, local_sem, halo_sems, one_send, one_recv, two_send, two_recv, pass_send,
):
    me = lax.axis_index("tm")
    region = lax.axis_index("region")
    barrier = pltpu.get_barrier_semaphore()
    for d in range(1, count):
        pl.semaphore_signal(barrier, inc=1, device_id=(lax.rem(me + d, count), region), device_id_type=MESH)
    small = [
        pltpu.make_async_copy(source, target, small_sems.at[i])
        for i, (source, target) in enumerate(
            [(library_hbm, library_ref), (owner_hbm, owner_ref), (order_hbm, order_ref), (channels_hbm, channels_ref)]
        )
    ]
    for copy in small:
        copy.start()
    load = pltpu.make_async_copy(x_ref, local, local_sem)
    load.start()
    for copy in small:
        copy.wait()

    taps = library_ref.shape[1]
    tiles = mine.shape[0]
    panel = library_ref[...]
    centred = panel - jnp.sum(panel, axis=1, keepdims=True) / taps
    normed = centred / jnp.sqrt(jnp.sum(centred * centred, axis=1, keepdims=True) + eps)
    normed = jnp.concatenate([normed, jnp.zeros((panel.shape[0], depth - taps), jnp.float32)], axis=1)
    mine[...] = normed.astype(jnp.bfloat16).reshape(tiles, 16, depth)

    half = tiles // 2
    chips = count // 2
    chip = me // 2
    core = me % 2
    sibling = chip * 2 + 1 - core
    seats = [v * chips // half for v in range(half)]
    holders = [seats[u // 2] * 2 + u % 2 for u in range(tiles)]
    seat = (chip * half + chips - 1) // chips
    holding = seat * chips // half == chip
    my_tile = jnp.minimum(seat, half - 1) * 2 + core

    pl.semaphore_wait(barrier, count - 1)
    left = lax.rem(me + count - 1, count)
    edge_copy = pltpu.make_async_remote_copy(
        src_ref=x_ref.at[:, pl.ds(0, depth)], dst_ref=halo, send_sem=halo_sems.at[0], recv_sem=halo_sems.at[1],
        device_id=(left, region), device_id_type=MESH,
    )
    edge_copy.start()

    def piece(u):
        return pltpu.make_async_remote_copy(
            src_ref=mine.at[u], dst_ref=got.at[me], send_sem=one_send.at[u], recv_sem=one_recv.at[me],
            device_id=(holders[u], region), device_id_type=MESH,
        )

    for u in range(tiles):
        @pl.when(me != holders[u])
        def _():
            piece(u).start()

    chans = x_ref.shape[0]
    blocks = x_ref.shape[1] // 128
    lane = lax.broadcasted_iota(jnp.int32, (1, 128), 1)
    low_half = lane < 64
    spread = lax.broadcasted_iota(jnp.int32, (offs, depth), 1) - lax.broadcasted_iota(jnp.int32, (offs, depth), 0)
    band = ((spread >= 0) & (spread < taps)).astype(jnp.float32).astype(jnp.bfloat16)
    width = 8

    def channel(c):
        x = [ext[c, m : m + blocks] for m in range(3)]
        y = [pltpu.roll(v, 64, 1) for v in x]
        columns = []
        for m in range(3):
            second = jnp.where(low_half, y[m], y[m + 1]) if m < 2 else y[m]
            columns.append(jnp.concatenate([x[m], second], axis=0).T)
        z = jnp.concatenate([columns[0], columns[1], columns[2][: rows_z - 256]], axis=0)
        z_ref[c] = z.astype(jnp.bfloat16)
        square = z * z
        high = square.astype(jnp.bfloat16)
        low = (square - high.astype(jnp.float32)).astype(jnp.bfloat16)

        def both(v):
            return jnp.concatenate([v[0:depth], v[offs : offs + depth]], axis=1)

        energy = jnp.dot(band, both(high), preferred_element_type=jnp.float32)
        energy = energy + jnp.dot(band, both(low), preferred_element_type=jnp.float32)
        inv_ref[c] = lax.rsqrt(energy + taps * water_level)

    def windows(first, last):
        def group(i, carry):
            for slot in range(width):
                channel(i * width + slot)
            return carry

        lax.fori_loop(first // width, last // width, group, 0)

    pair_lists(steps, regions, region, order_ref, channels_ref, list_ref)
    load.wait()

    def lay_out(i, carry):
        at = pl.ds(pl.multiple_of(i * 16, 16), 16)
        ext[at, 0:blocks] = local[at, :].astype(jnp.float32).reshape(16, blocks, 128)
        return carry

    lax.fori_loop(0, chans // 16, lay_out, 0)
    rest = chans // 16 * 16
    if rest < chans:
        ext[rest:chans, 0:blocks] = local[rest:chans, :].astype(jnp.float32).reshape(chans - rest, blocks, 128)
    edge_copy.wait()
    inside = (me < count - 1) & (lax.broadcasted_iota(jnp.int32, (1, depth), 1) < taps - 1)
    for i in range(0, chans, 16):
        end = min(i + 16, chans)
        rim = jnp.where(inside, halo[i:end].astype(jnp.float32), 0.0)
        ext[i:end, blocks : blocks + 2] = rim.reshape(end - i, 2, 128)
    early = chans // 4 // width * width
    late = chans * 3 // 4 // width * width
    windows(0, early)

    for u in range(tiles):
        @pl.when(me != holders[u])
        def _():
            piece(u).wait_send()

    def spread_copy(e):
        peer = sibling if e == 0 else lax.rem(chip + e, chips) * 2 + core
        return pltpu.make_async_remote_copy(
            src_ref=sel, dst_ref=full.at[my_tile], send_sem=two_send.at[e], recv_sem=two_recv.at[my_tile],
            device_id=(peer, region), device_id_type=MESH,
        )

    @pl.when(holding)
    def _():
        for i in range(count):
            @pl.when(me != i)
            def _():
                pltpu.make_async_remote_copy(
                    src_ref=mine.at[0], dst_ref=got.at[i], send_sem=one_send.at[0], recv_sem=one_recv.at[i],
                    device_id=(left, region), device_id_type=MESH,
                ).wait_recv()
        got[me] = mine[my_tile]
        for s in range(steps):
            sel[s] = got[owner_ref[s]]
        full[my_tile] = sel[...]
        for e in range(1, chips):
            spread_copy(e).start()
        spread_copy(0).start()

    windows(early, late)

    def pass_copy(v):
        u = 2 * v + core
        return pltpu.make_async_remote_copy(
            src_ref=full.at[u], dst_ref=full.at[u], send_sem=pass_send.at[v], recv_sem=two_recv.at[u],
            device_id=(sibling, region), device_id_type=MESH,
        )

    for v in range(half):
        @pl.when(chip != seats[v])
        def _():
            pass_copy(v).wait_recv()
            pass_copy(v).start()

    windows(late, chans)

    for v in range(half):
        u = 2 * v + 1 - core
        pltpu.make_async_remote_copy(
            src_ref=sel, dst_ref=full.at[u], send_sem=two_send.at[0], recv_sem=two_recv.at[u],
            device_id=(sibling, region), device_id_type=MESH,
        ).wait_recv()

    taps_ref[0 : tiles * steps * 16] = full[...].astype(jnp.float32).reshape(tiles * steps * 16, depth)
    taps_ref[tiles * steps * 16 :] = jnp.zeros((8, depth), jnp.float32)

    @pl.when(holding)
    def _():
        for e in range(chips):
            spread_copy(e).wait_send()

    for v in range(half):
        @pl.when(chip != seats[v])
        def _():
            pass_copy(v).wait_send()


def pair_kernel(which, list_ref, z_ref, inv_ref, taps_ref, out_ref, acc_ref):
    held = out_ref.shape[0]
    total = list_ref[which, 0, list_ref.shape[2] - 1]
    acc_ref[...] = jnp.zeros_like(acc_ref)

    def shifted(row):
        base = jnp.broadcast_to(taps_ref[pl.ds(row, 1)], (offs, depth))
        return pltpu.roll(base, 0, 1, stride=1, stride_axis=0)

    def entry(e):
        codes = [list_ref[which, 0, 2 * e + i] for i in range(2)]
        matrix = jnp.concatenate([shifted(codes[i] & 1023) for i in range(2)], axis=0).astype(jnp.bfloat16)
        col = (codes[0] >> 10) & 127
        window = jnp.concatenate([z_ref[col, 0:depth], z_ref[col, offs : offs + depth]], axis=1)
        product = jnp.dot(matrix, window, preferred_element_type=jnp.float32)
        scale = inv_ref[col]
        return [(codes[i] >> 17, product[i * offs : (i + 1) * offs] * scale) for i in range(2)]

    def group(i, carry):
        done = [entry(i * unroll + u) for u in range(unroll)]
        for both in done:
            for template, value in both:
                acc_ref[template] += value
        return carry

    lax.fori_loop(0, (total + unroll - 1) // unroll, group, 0)
    out_ref[...] = acc_ref[:held].astype(out_ref.dtype)


def finish_kernel(total_time, count, *refs):
    *parts, out_ref, stacked, power_sent, power_got, p_send, p_recv = refs
    me = lax.axis_index("tm")
    region = lax.axis_index("region")
    barrier = pltpu.get_barrier_semaphore()
    for d in range(1, count):
        pl.semaphore_signal(barrier, inc=1, device_id=(lax.rem(me + d, count), region), device_id_type=MESH)
    held = out_ref.shape[0]
    lane = lax.broadcasted_iota(jnp.int32, (1, 128), 1)
    power = jnp.zeros((1, 128), jnp.float32)
    for at in range(held):
        value = parts[-1][at]
        for other in parts[:-1]:
            value = value + other[at].astype(jnp.float32)
        stacked[at] = value
        total = jnp.sum(jnp.sum(value * value, axis=0, keepdims=True), axis=1, keepdims=True)
        power = power + jnp.where(lane == at, total, 0.0)
    power_sent[...] = power
    pl.semaphore_wait(barrier, count - 1)
    copies = []
    for d in range(1, count):
        copy = pltpu.make_async_remote_copy(
            src_ref=power_sent, dst_ref=power_got.at[d - 1], send_sem=p_send.at[d - 1], recv_sem=p_recv.at[d - 1],
            device_id=(lax.rem(me + d, count), region), device_id_type=MESH,
        )
        copy.start()
        copies.append(copy)
    for at in range(held):
        value = stacked[at]
        turned = jnp.concatenate([value[:, :128], value[:, 128:]], axis=0).T
        out_ref[at] = jnp.concatenate([turned[:64], turned[64:]], axis=1)
    for copy in copies:
        copy.wait()
    power = power + jnp.sum(power_got[...], axis=0)
    factor = lax.rsqrt(power / total_time + eps)
    for at in range(held):
        one = jnp.sum(jnp.where(lane == at, factor, 0.0), axis=1, keepdims=True)
        out_ref[at] = out_ref[at] * one


def body(waveform, station_order, library, owner, channels):
    chans, time_local = waveform.shape
    blocks = time_local // 128
    steps, templates, used = channels.shape
    tap_count = library.shape[2]
    count = lax.axis_size("tm")
    regions = lax.axis_size("region")
    per = templates // regions
    held = steps * per
    all_templates = steps * templates
    pairs = all_templates * used
    tiles = templates * used // 16
    lanes = time_local // offs

    vmem = pl.BlockSpec(memory_space=pltpu.VMEM)
    smem = pl.BlockSpec(memory_space=pltpu.SMEM)
    dma = pltpu.SemaphoreType.DMA
    length = -(-(held * used + chans + 2 * unroll + 1) // 128) * 128
    z, inv_scale, taps, lists = pl.pallas_call(
        functools.partial(prepare_kernel, steps, count, regions),
        out_shape=[
            jax.ShapeDtypeStruct((chans, rows_z, 128), jnp.bfloat16),
            jax.ShapeDtypeStruct((chans, offs, lanes), jnp.float32),
            jax.ShapeDtypeStruct((pairs + 8, depth), jnp.float32),
            jax.ShapeDtypeStruct((regions, 1, length), jnp.int32),
        ],
        in_specs=[pl.BlockSpec(memory_space=pltpu.HBM)] * 5,
        out_specs=[vmem] * 4,
        scratch_shapes=[
            pltpu.SMEM((steps,), jnp.int32),
            pltpu.VMEM((templates * used, tap_count), jnp.float32),
            pltpu.VMEM((1, chans), jnp.int32),
            pltpu.VMEM((all_templates, used), jnp.int32),
            dma((4,)),
            pltpu.VMEM((tiles, 16, depth), jnp.bfloat16),
            pltpu.VMEM((count, 16, depth), jnp.bfloat16),
            pltpu.VMEM((steps, 16, depth), jnp.bfloat16),
            pltpu.VMEM((tiles, steps, 16, depth), jnp.bfloat16),
            pltpu.VMEM((chans, depth), jnp.bfloat16),
            pltpu.VMEM((chans, time_local), jnp.bfloat16),
            pltpu.VMEM((chans, blocks + 8, 128), jnp.float32),
            dma,
            dma((2,)),
            dma((tiles,)),
            dma((count,)),
            dma((count // 2,)),
            dma((tiles,)),
            dma((tiles // 2,)),
        ],
        compiler_params=pltpu.CompilerParams(collective_id=0, has_side_effects=True, vmem_limit_bytes=16 * 2**20),
        name="prepare",
    )(*[pltpu.with_memory_space_constraint(v, pltpu.HBM) for v in (
        owner, library.reshape(templates * used, tap_count), waveform,
        station_order.reshape(1, chans), channels.reshape(all_templates, used),
    )])

    def partial_sums(which, dtype):
        return pl.pallas_call(
            functools.partial(pair_kernel, which),
            out_shape=jax.ShapeDtypeStruct((held, offs, lanes), dtype),
            in_specs=[smem, vmem, vmem, vmem],
            out_specs=vmem,
            scratch_shapes=[pltpu.VMEM((held + 1, offs, lanes), jnp.float32)],
            compiler_params=pltpu.CompilerParams(vmem_limit_bytes=16 * 2**20),
            cost_estimate=pl.CostEstimate(flops=held * used * offs * depth * lanes, bytes_accessed=12 * 2**20, transcendentals=0),
            name="pairs",
        )(lists, z, inv_scale, taps)

    parts = []
    for d in range(1, regions):
        part = partial_sums(d - 1, jnp.bfloat16)
        parts.append(lax.ppermute(part, "region", [(i, (i + d) % regions) for i in range(regions)]))
    parts.append(partial_sums(regions - 1, jnp.float32))

    result = pl.pallas_call(
        functools.partial(finish_kernel, time_local * count, count),
        out_shape=jax.ShapeDtypeStruct((held, blocks, 128), jnp.float32),
        in_specs=[vmem] * regions,
        out_specs=vmem,
        scratch_shapes=[
            pltpu.VMEM((held, offs, lanes), jnp.float32),
            pltpu.VMEM((1, 128), jnp.float32),
            pltpu.VMEM((count - 1, 1, 128), jnp.float32),
            dma((count - 1,)),
            dma((count - 1,)),
        ],
        compiler_params=pltpu.CompilerParams(collective_id=1, has_side_effects=True, vmem_limit_bytes=16 * 2**20),
        name="finish",
    )(*parts)
    return result.reshape(steps, per, time_local)


def solution(mesh):
    in_specs = (P("region", "tm"), P("region"), P("tm", None, None), P(), P())
    out_specs = P(None, "region", "tm")
    return jax.shard_map(body, mesh=mesh, in_specs=in_specs, out_specs=out_specs, check_vma=False)
```

```python
import functools
import jax
import jax.numpy as jnp
from jax import lax
from jax.experimental import pallas as pl
from jax.experimental.pallas import tpu as pltpu
from jax.sharding import PartitionSpec as P

water_level = 4.0
eps = 1e-06
offs = 32
depth = 256
rows_z = 288
unroll = 32
MESH = pl.DeviceIdType.MESH


def pair_lists(steps, regions, region, order_ref, channels_ref, list_ref):
    rows, used = channels_ref.shape
    templates = rows // steps
    per = templates // regions
    held = steps * per
    chans = order_ref.shape[1]
    length = list_ref.shape[2]
    f32, bf16 = jnp.float32, jnp.bfloat16
    order = order_ref[...]
    table = channels_ref[...]
    hit = jnp.zeros((rows, chans), jnp.int32)
    place = jnp.zeros((rows, chans), jnp.int32)
    for j in range(used):
        same = jnp.broadcast_to(table[:, j : j + 1], (rows, chans)) == order
        hit = hit + jnp.where(same, 1, 0)
        place = place + jnp.where(same, j, 0)
    one = lax.broadcasted_iota(jnp.int32, (rows, rows), 0)
    two = lax.broadcasted_iota(jnp.int32, (rows, rows), 1)
    together = one % templates // per == two % templates // per

    def ones(mask):
        return jnp.where(mask, 1.0, 0.0).astype(bf16)

    hits = hit.astype(f32)
    rank = jnp.dot(ones(together & (two < one)), hits.astype(bf16), preferred_element_type=f32)
    amount = jnp.dot(ones(together), hits.astype(bf16), preferred_element_type=f32)
    entries = jnp.floor((amount + 1) * 0.5)
    before = ones(lax.broadcasted_iota(jnp.int32, (chans, chans), 0) < lax.broadcasted_iota(jnp.int32, (chans, chans), 1))
    first = jnp.dot(entries.astype(bf16), before, preferred_element_type=f32)
    position = jnp.where(hits > 0, 2 * first + rank, -1.0)
    row = lax.broadcasted_iota(jnp.int32, (rows, chans), 0)
    step = row // templates
    inner = row % templates * used + place
    source = (inner // 16 * steps + step) * 16 + inner % 16
    target = step * per + row % templates % per
    column = lax.broadcasted_iota(jnp.int32, (rows, chans), 1)
    empty = held * 2**17 + rows * used
    code = (target * 2**17 + column * 2**10 + source - empty).astype(f32)
    blank = jnp.zeros((rows, 128 - chans), f32)
    position = jnp.concatenate([position, blank - 1], axis=1).T
    code = jnp.concatenate([code, blank], axis=1).T
    total = jnp.sum(entries, axis=1, keepdims=True)
    for g in range(regions):
        mine = [s * templates + g * per + k for s in range(steps) for k in range(per)]
        for base in range(0, length, 128):
            index = (lax.broadcasted_iota(jnp.int32, (128, 128), 1) + base).astype(f32)
            found = jnp.zeros((128, 128), f32)
            for t in mine:
                found = found + jnp.where(position[:, t : t + 1] == index, code[:, t : t + 1], 0.0)
            line = jnp.sum(found, axis=0, keepdims=True).astype(jnp.int32) + empty
            if base + 128 == length:
                last = lax.broadcasted_iota(jnp.int32, (1, 128), 1) == 127
                line = jnp.where(last, total[mine[0] : mine[0] + 1].astype(jnp.int32), line)
            list_ref[lax.rem(g - region - 1 + 2 * regions, regions), 0:1, base : base + 128] = line


def prepare_kernel(
    steps, count, regions, owner_hbm, library_hbm, x_ref, order_hbm, channels_hbm, z_ref, inv_ref, taps_ref, list_ref,
    owner_ref, library_ref, order_ref, channels_ref, small_sems, mine, got, sel, full, halo, local, ext, turned, local_sem, halo_sems, one_send, one_recv, two_send, two_recv, pass_send,
):
    me = lax.axis_index("tm")
    region = lax.axis_index("region")
    barrier = pltpu.get_barrier_semaphore()
    for d in range(1, count):
        pl.semaphore_signal(barrier, inc=1, device_id=(lax.rem(me + d, count), region), device_id_type=MESH)
    small = [
        pltpu.make_async_copy(source, target, small_sems.at[i])
        for i, (source, target) in enumerate(
            [(library_hbm, library_ref), (owner_hbm, owner_ref), (order_hbm, order_ref), (channels_hbm, channels_ref)]
        )
    ]
    for copy in small:
        copy.start()
    load = pltpu.make_async_copy(x_ref, local, local_sem)
    load.start()
    for copy in small:
        copy.wait()

    taps = library_ref.shape[1]
    tiles = mine.shape[0]
    panel = library_ref[...]
    centred = panel - jnp.sum(panel, axis=1, keepdims=True) / taps
    normed = centred / jnp.sqrt(jnp.sum(centred * centred, axis=1, keepdims=True) + eps)
    normed = jnp.concatenate([normed, jnp.zeros((panel.shape[0], depth - taps), jnp.float32)], axis=1)
    mine[...] = normed.astype(jnp.bfloat16).reshape(tiles, 16, depth)

    half = tiles // 2
    chips = count // 2
    chip = me // 2
    core = me % 2
    sibling = chip * 2 + 1 - core
    seats = [v * chips // half for v in range(half)]
    holders = [seats[u // 2] * 2 + u % 2 for u in range(tiles)]
    seat = (chip * half + chips - 1) // chips
    holding = seat * chips // half == chip
    my_tile = jnp.minimum(seat, half - 1) * 2 + core

    pl.semaphore_wait(barrier, count - 1)
    left = lax.rem(me + count - 1, count)
    edge_copy = pltpu.make_async_remote_copy(
        src_ref=x_ref.at[:, pl.ds(0, depth)], dst_ref=halo, send_sem=halo_sems.at[0], recv_sem=halo_sems.at[1],
        device_id=(left, region), device_id_type=MESH,
    )
    edge_copy.start()

    def piece(u):
        return pltpu.make_async_remote_copy(
            src_ref=mine.at[u], dst_ref=got.at[me], send_sem=one_send.at[u], recv_sem=one_recv.at[me],
            device_id=(holders[u], region), device_id_type=MESH,
        )

    for u in range(tiles):
        @pl.when(me != holders[u])
        def _():
            piece(u).start()

    chans = x_ref.shape[0]
    blocks = x_ref.shape[1] // 128
    lane = lax.broadcasted_iota(jnp.int32, (1, 128), 1)
    low_half = lane < 64
    spread = lax.broadcasted_iota(jnp.int32, (offs, depth), 1) - lax.broadcasted_iota(jnp.int32, (offs, depth), 0)
    band = ((spread >= 0) & (spread < taps)).astype(jnp.float32).astype(jnp.bfloat16)
    width = 16 if chans % 16 == 0 else 8

    def channel(c, tips):
        y = [turned[c, m : m + blocks] for m in range(3)]
        columns = [
            jnp.concatenate([ext[c, m : m + blocks], jnp.where(low_half, y[m], y[m + 1])], axis=0).T for m in range(2)
        ]
        last = pltpu.roll(columns[0][:8], 126, 1)
        last = jnp.where(lane % 64 == 62, pltpu.roll(columns[1][:8], 127, 1), last)
        last = jnp.where(lane == 63, pltpu.roll(tips[0], lax.rem(191 - c, 128), 1), last)
        last = jnp.where(lane == 127, pltpu.roll(tips[1], 127 - c, 1), last)
        z = jnp.concatenate(columns + [last, jnp.zeros((rows_z - 264, 128), jnp.float32)], axis=0)
        z_ref[c] = z.astype(jnp.bfloat16)
        square = z * z
        high = square.astype(jnp.bfloat16)
        low = (square - high.astype(jnp.float32)).astype(jnp.bfloat16)

        def both(v):
            return jnp.concatenate([v[0:depth], v[offs : offs + depth]], axis=1)

        energy = jnp.dot(band, both(high), preferred_element_type=jnp.float32)
        energy = energy + jnp.dot(band, both(low), preferred_element_type=jnp.float32)
        inv_ref[c] = lax.rsqrt(energy + taps * water_level)

    def windows(first, last, tips):
        def group(i, carry):
            for slot in range(width):
                channel(i * width + slot, tips)
            return carry

        lax.fori_loop(first // width, last // width, group, 0)

    pair_lists(steps, regions, region, order_ref, channels_ref, list_ref)
    load.wait()

    def place(at, row, value):
        ext[at, row : row + value.shape[1]] = value
        turned[at, row : row + value.shape[1]] = pltpu.roll(value, 64, 2)

    def lay_out(i, carry):
        at = pl.ds(pl.multiple_of(i * 16, 16), 16)
        place(at, 0, local[at, :].astype(jnp.float32).reshape(16, blocks, 128))
        return carry

    lax.fori_loop(0, chans // 16, lay_out, 0)
    rest = chans // 16 * 16
    if rest < chans:
        place(pl.ds(rest, chans - rest), 0, local[rest:chans, :].astype(jnp.float32).reshape(chans - rest, blocks, 128))
    for u in range(tiles):
        @pl.when(me != holders[u])
        def _():
            piece(u).wait_send()

    def spread_copy(e):
        peer = sibling if e == 0 else lax.rem(chip + e, chips) * 2 + core
        return pltpu.make_async_remote_copy(
            src_ref=sel, dst_ref=full.at[my_tile], send_sem=two_send.at[e], recv_sem=two_recv.at[my_tile],
            device_id=(peer, region), device_id_type=MESH,
        )

    @pl.when(holding)
    def _():
        for i in range(count):
            @pl.when(me != i)
            def _():
                pltpu.make_async_remote_copy(
                    src_ref=mine.at[0], dst_ref=got.at[i], send_sem=one_send.at[0], recv_sem=one_recv.at[i],
                    device_id=(left, region), device_id_type=MESH,
                ).wait_recv()
        got[me] = mine[my_tile]
        for s in range(steps):
            sel[s] = got[owner_ref[s]]
        full[my_tile] = sel[...]
        for e in range(1, chips):
            spread_copy(e).start()
        spread_copy(0).start()

    edge_copy.wait()
    inside = (me < count - 1) & (lax.broadcasted_iota(jnp.int32, (1, depth), 1) < taps - 1)
    rims = []
    for i in range(0, chans, 16):
        end = min(i + 16, chans)
        rim = jnp.where(inside, halo[i:end].astype(jnp.float32), 0.0)
        rims.append(rim[:, 128:])
        place(pl.ds(i, end - i), blocks, rim.reshape(end - i, 2, 128))
    tips = jnp.concatenate(rims + [jnp.zeros((128 - chans, 128), jnp.float32)], axis=0).T
    tips = [tips[0:8], tips[64:72]]
    late = chans * 5 // 6 // width * width
    windows(0, late, tips)

    def pass_copy(v):
        u = 2 * v + core
        return pltpu.make_async_remote_copy(
            src_ref=full.at[u], dst_ref=full.at[u], send_sem=pass_send.at[v], recv_sem=two_recv.at[u],
            device_id=(sibling, region), device_id_type=MESH,
        )

    for v in range(half):
        @pl.when(chip != seats[v])
        def _():
            pass_copy(v).wait_recv()
            pass_copy(v).start()

    windows(late, chans, tips)

    for v in range(half):
        u = 2 * v + 1 - core
        pltpu.make_async_remote_copy(
            src_ref=sel, dst_ref=full.at[u], send_sem=two_send.at[0], recv_sem=two_recv.at[u],
            device_id=(sibling, region), device_id_type=MESH,
        ).wait_recv()

    taps_ref[0 : tiles * steps * 16] = full[...].astype(jnp.float32).reshape(tiles * steps * 16, depth)
    taps_ref[tiles * steps * 16 :] = jnp.zeros((8, depth), jnp.float32)

    @pl.when(holding)
    def _():
        for e in range(chips):
            spread_copy(e).wait_send()

    for v in range(half):
        @pl.when(chip != seats[v])
        def _():
            pass_copy(v).wait_send()


def pair_kernel(which, list_ref, z_ref, inv_ref, taps_ref, out_ref, acc_ref):
    held = out_ref.shape[0]
    total = list_ref[which, 0, list_ref.shape[2] - 1]
    acc_ref[...] = jnp.zeros_like(acc_ref)

    def shifted(row):
        base = jnp.broadcast_to(taps_ref[pl.ds(row, 1)], (offs, depth))
        return pltpu.roll(base, 0, 1, stride=1, stride_axis=0)

    def entry(e):
        codes = [list_ref[which, 0, 2 * e + i] for i in range(2)]
        matrix = jnp.concatenate([shifted(codes[i] & 1023) for i in range(2)], axis=0).astype(jnp.bfloat16)
        col = (codes[0] >> 10) & 127
        window = jnp.concatenate([z_ref[col, 0:depth], z_ref[col, offs : offs + depth]], axis=1)
        product = jnp.dot(matrix, window, preferred_element_type=jnp.float32)
        scale = inv_ref[col]
        return [(codes[i] >> 17, product[i * offs : (i + 1) * offs] * scale) for i in range(2)]

    def group(i, carry):
        done = [entry(i * unroll + u) for u in range(unroll)]
        for both in done:
            for template, value in both:
                acc_ref[template] += value
        return carry

    lax.fori_loop(0, (total + unroll - 1) // unroll, group, 0)
    out_ref[...] = acc_ref[:held].astype(out_ref.dtype)


def finish_kernel(total_time, count, *refs):
    *parts, out_ref, stacked, power_sent, power_got, p_send, p_recv = refs
    me = lax.axis_index("tm")
    region = lax.axis_index("region")
    barrier = pltpu.get_barrier_semaphore()
    for d in range(1, count):
        pl.semaphore_signal(barrier, inc=1, device_id=(lax.rem(me + d, count), region), device_id_type=MESH)
    held = out_ref.shape[0]
    lane = lax.broadcasted_iota(jnp.int32, (1, 128), 1)
    power = jnp.zeros((1, 128), jnp.float32)
    for at in range(held):
        value = parts[-1][at]
        for other in parts[:-1]:
            value = value + other[at].astype(jnp.float32)
        stacked[at] = value
        total = jnp.sum(jnp.sum(value * value, axis=0, keepdims=True), axis=1, keepdims=True)
        power = power + jnp.where(lane == at, total, 0.0)
    power_sent[...] = power
    pl.semaphore_wait(barrier, count - 1)
    copies = []
    for d in range(1, count):
        copy = pltpu.make_async_remote_copy(
            src_ref=power_sent, dst_ref=power_got.at[d - 1], send_sem=p_send.at[d - 1], recv_sem=p_recv.at[d - 1],
            device_id=(lax.rem(me + d, count), region), device_id_type=MESH,
        )
        copy.start()
        copies.append(copy)
    for at in range(held):
        value = stacked[at]
        turned = jnp.concatenate([value[:, :128], value[:, 128:]], axis=0).T
        out_ref[at] = jnp.concatenate([turned[:64], turned[64:]], axis=1)
    for copy in copies:
        copy.wait()
    power = power + jnp.sum(power_got[...], axis=0)
    factor = lax.rsqrt(power / total_time + eps)
    for at in range(held):
        one = jnp.sum(jnp.where(lane == at, factor, 0.0), axis=1, keepdims=True)
        out_ref[at] = out_ref[at] * one


def body(waveform, station_order, library, owner, channels):
    chans, time_local = waveform.shape
    blocks = time_local // 128
    steps, templates, used = channels.shape
    tap_count = library.shape[2]
    count = lax.axis_size("tm")
    regions = lax.axis_size("region")
    per = templates // regions
    held = steps * per
    all_templates = steps * templates
    pairs = all_templates * used
    tiles = templates * used // 16
    lanes = time_local // offs

    vmem = pl.BlockSpec(memory_space=pltpu.VMEM)
    smem = pl.BlockSpec(memory_space=pltpu.SMEM)
    dma = pltpu.SemaphoreType.DMA
    length = -(-(held * used + chans + 2 * unroll + 1) // 128) * 128
    z, inv_scale, taps, lists = pl.pallas_call(
        functools.partial(prepare_kernel, steps, count, regions),
        out_shape=[
            jax.ShapeDtypeStruct((chans, rows_z, 128), jnp.bfloat16),
            jax.ShapeDtypeStruct((chans, offs, lanes), jnp.float32),
            jax.ShapeDtypeStruct((pairs + 8, depth), jnp.float32),
            jax.ShapeDtypeStruct((regions, 1, length), jnp.int32),
        ],
        in_specs=[pl.BlockSpec(memory_space=pltpu.HBM)] * 5,
        out_specs=[vmem] * 4,
        scratch_shapes=[
            pltpu.SMEM((steps,), jnp.int32),
            pltpu.VMEM((templates * used, tap_count), jnp.float32),
            pltpu.VMEM((1, chans), jnp.int32),
            pltpu.VMEM((all_templates, used), jnp.int32),
            dma((4,)),
            pltpu.VMEM((tiles, 16, depth), jnp.bfloat16),
            pltpu.VMEM((count, 16, depth), jnp.bfloat16),
            pltpu.VMEM((steps, 16, depth), jnp.bfloat16),
            pltpu.VMEM((tiles, steps, 16, depth), jnp.bfloat16),
            pltpu.VMEM((chans, depth), jnp.bfloat16),
            pltpu.VMEM((chans, time_local), jnp.bfloat16),
            pltpu.VMEM((chans, blocks + 8, 128), jnp.float32),
            pltpu.VMEM((chans, blocks + 8, 128), jnp.float32),
            dma,
            dma((2,)),
            dma((tiles,)),
            dma((count,)),
            dma((count // 2,)),
            dma((tiles,)),
            dma((tiles // 2,)),
        ],
        compiler_params=pltpu.CompilerParams(collective_id=0, has_side_effects=True, vmem_limit_bytes=28 * 2**20),
        name="prepare",
    )(*[pltpu.with_memory_space_constraint(v, pltpu.HBM) for v in (
        owner, library.reshape(templates * used, tap_count), waveform,
        station_order.reshape(1, chans), channels.reshape(all_templates, used),
    )])

    def partial_sums(which, dtype):
        return pl.pallas_call(
            functools.partial(pair_kernel, which),
            out_shape=jax.ShapeDtypeStruct((held, offs, lanes), dtype),
            in_specs=[smem, vmem, vmem, vmem],
            out_specs=vmem,
            scratch_shapes=[pltpu.VMEM((held + 1, offs, lanes), jnp.float32)],
            compiler_params=pltpu.CompilerParams(vmem_limit_bytes=16 * 2**20),
            cost_estimate=pl.CostEstimate(flops=held * used * offs * depth * lanes, bytes_accessed=12 * 2**20, transcendentals=0),
            name="pairs",
        )(lists, z, inv_scale, taps)

    parts = []
    for d in range(1, regions):
        part = partial_sums(d - 1, jnp.bfloat16)
        parts.append(lax.ppermute(part, "region", [(i, (i + d) % regions) for i in range(regions)]))
    parts.append(partial_sums(regions - 1, jnp.float32))

    result = pl.pallas_call(
        functools.partial(finish_kernel, time_local * count, count),
        out_shape=jax.ShapeDtypeStruct((held, blocks, 128), jnp.float32),
        in_specs=[vmem] * regions,
        out_specs=vmem,
        scratch_shapes=[
            pltpu.VMEM((held, offs, lanes), jnp.float32),
            pltpu.VMEM((1, 128), jnp.float32),
            pltpu.VMEM((count - 1, 1, 128), jnp.float32),
            dma((count - 1,)),
            dma((count - 1,)),
        ],
        compiler_params=pltpu.CompilerParams(collective_id=1, has_side_effects=True, vmem_limit_bytes=16 * 2**20),
        name="finish",
    )(*parts)
    return result.reshape(steps, per, time_local)


def solution(mesh):
    in_specs = (P("region", "tm"), P("region"), P("tm", None, None), P(), P())
    out_specs = P(None, "region", "tm")
    return jax.shard_map(body, mesh=mesh, in_specs=in_specs, out_specs=out_specs, check_vma=False)
```

```python
import functools
import jax
import jax.numpy as jnp
from jax import lax
from jax.experimental import pallas as pl
from jax.experimental.pallas import tpu as pltpu
from jax.sharding import PartitionSpec as P

water_level = 4.0
eps = 1e-06
offs = 32
depth = 256
rows_z = 288
unroll = 64
MESH = pl.DeviceIdType.MESH


def pair_lists(steps, regions, region, order_ref, channels_ref, list_ref):
    rows, used = channels_ref.shape
    templates = rows // steps
    per = templates // regions
    held = steps * per
    chans = order_ref.shape[1]
    length = list_ref.shape[2]
    f32, bf16 = jnp.float32, jnp.bfloat16
    order = order_ref[...]
    table = channels_ref[...]
    hit = jnp.zeros((rows, chans), jnp.int32)
    place = jnp.zeros((rows, chans), jnp.int32)
    for j in range(used):
        same = jnp.broadcast_to(table[:, j : j + 1], (rows, chans)) == order
        hit = hit + jnp.where(same, 1, 0)
        place = place + jnp.where(same, j, 0)
    one = lax.broadcasted_iota(jnp.int32, (rows, rows), 0)
    two = lax.broadcasted_iota(jnp.int32, (rows, rows), 1)
    together = one % templates // per == two % templates // per

    def ones(mask):
        return jnp.where(mask, 1.0, 0.0).astype(bf16)

    hits = hit.astype(f32)
    rank = jnp.dot(ones(together & (two < one)), hits.astype(bf16), preferred_element_type=f32)
    amount = jnp.dot(ones(together), hits.astype(bf16), preferred_element_type=f32)
    entries = jnp.floor((amount + 1) * 0.5)
    before = ones(lax.broadcasted_iota(jnp.int32, (chans, chans), 0) < lax.broadcasted_iota(jnp.int32, (chans, chans), 1))
    first = jnp.dot(entries.astype(bf16), before, preferred_element_type=f32)
    position = jnp.where(hits > 0, 2 * first + rank, -1.0)
    row = lax.broadcasted_iota(jnp.int32, (rows, chans), 0)
    step = row // templates
    inner = row % templates * used + place
    source = (inner // 16 * steps + step) * 16 + inner % 16
    target = step * per + row % templates % per
    column = lax.broadcasted_iota(jnp.int32, (rows, chans), 1)
    empty = held * 2**17 + rows * used
    code = (target * 2**17 + column * 2**10 + source - empty).astype(f32)
    blank = jnp.zeros((rows, 128 - chans), f32)
    position = jnp.concatenate([position, blank - 1], axis=1).T
    code = jnp.concatenate([code, blank], axis=1).T
    total = jnp.sum(entries, axis=1, keepdims=True)
    for g in range(regions):
        mine = [s * templates + g * per + k for s in range(steps) for k in range(per)]
        for base in range(0, length, 128):
            index = (lax.broadcasted_iota(jnp.int32, (128, 128), 1) + base).astype(f32)
            found = jnp.zeros((128, 128), f32)
            for t in mine:
                found = found + jnp.where(position[:, t : t + 1] == index, code[:, t : t + 1], 0.0)
            line = jnp.sum(found, axis=0, keepdims=True).astype(jnp.int32) + empty
            if base + 128 == length:
                last = lax.broadcasted_iota(jnp.int32, (1, 128), 1) == 127
                line = jnp.where(last, total[mine[0] : mine[0] + 1].astype(jnp.int32), line)
            list_ref[lax.rem(g - region - 1 + 2 * regions, regions), 0:1, base : base + 128] = line


def prepare_kernel(
    steps, count, regions, owner_hbm, library_hbm, x_ref, order_hbm, channels_hbm, z_ref, inv_ref, taps_ref, list_ref,
    owner_ref, library_ref, order_ref, channels_ref, small_sems, mine, got, sel, full, halo, local, ext, turned, local_sem, halo_sems, one_send, one_recv, two_send, two_recv, pass_send,
):
    me = lax.axis_index("tm")
    region = lax.axis_index("region")
    barrier = pltpu.get_barrier_semaphore()
    for d in range(1, count):
        pl.semaphore_signal(barrier, inc=1, device_id=(lax.rem(me + d, count), region), device_id_type=MESH)
    small = [
        pltpu.make_async_copy(source, target, small_sems.at[i])
        for i, (source, target) in enumerate(
            [(library_hbm, library_ref), (owner_hbm, owner_ref), (order_hbm, order_ref), (channels_hbm, channels_ref)]
        )
    ]
    for copy in small:
        copy.start()
    load = pltpu.make_async_copy(x_ref, local, local_sem)
    load.start()
    for copy in small:
        copy.wait()

    taps = library_ref.shape[1]
    tiles = mine.shape[0]
    panel = library_ref[...]
    centred = panel - jnp.sum(panel, axis=1, keepdims=True) / taps
    normed = centred / jnp.sqrt(jnp.sum(centred * centred, axis=1, keepdims=True) + eps)
    normed = jnp.concatenate([normed, jnp.zeros((panel.shape[0], depth - taps), jnp.float32)], axis=1)
    mine[...] = normed.astype(jnp.bfloat16).reshape(tiles, 16, depth)

    half = tiles // 2
    chips = count // 2
    chip = me // 2
    core = me % 2
    sibling = chip * 2 + 1 - core
    seats = [v * chips // half for v in range(half)]
    holders = [seats[u // 2] * 2 + u % 2 for u in range(tiles)]
    seat = (chip * half + chips - 1) // chips
    holding = seat * chips // half == chip
    my_tile = jnp.minimum(seat, half - 1) * 2 + core

    pl.semaphore_wait(barrier, count - 1)
    left = lax.rem(me + count - 1, count)
    edge_copy = pltpu.make_async_remote_copy(
        src_ref=x_ref.at[:, pl.ds(0, depth)], dst_ref=halo, send_sem=halo_sems.at[0], recv_sem=halo_sems.at[1],
        device_id=(left, region), device_id_type=MESH,
    )

    def piece(u):
        return pltpu.make_async_remote_copy(
            src_ref=mine.at[u], dst_ref=got.at[me], send_sem=one_send.at[u], recv_sem=one_recv.at[me],
            device_id=(holders[u], region), device_id_type=MESH,
        )

    for u in range(tiles):
        @pl.when(me != holders[u])
        def _():
            piece(u).start()

    @pl.when(me > 0)
    def _():
        edge_copy.start()

    chans = x_ref.shape[0]
    blocks = x_ref.shape[1] // 128
    lane = lax.broadcasted_iota(jnp.int32, (1, 128), 1)
    low_half = lane < 64
    spread = lax.broadcasted_iota(jnp.int32, (offs, depth), 1) - lax.broadcasted_iota(jnp.int32, (offs, depth), 0)
    band = ((spread >= 0) & (spread < taps)).astype(jnp.float32).astype(jnp.bfloat16)
    width = 16 if chans % 16 == 0 else 8

    def channel(c, tips):
        y = [turned[c, m : m + blocks] for m in range(3)]
        columns = [
            jnp.concatenate([ext[c, m : m + blocks], jnp.where(low_half, y[m], y[m + 1])], axis=0).T for m in range(2)
        ]
        last = pltpu.roll(columns[0][:8], 126, 1)
        last = jnp.where(lane % 64 == 62, pltpu.roll(columns[1][:8], 127, 1), last)
        last = jnp.where(lane == 63, pltpu.roll(tips[0], lax.rem(191 - c, 128), 1), last)
        last = jnp.where(lane == 127, pltpu.roll(tips[1], 127 - c, 1), last)
        z = jnp.concatenate(columns + [last, jnp.zeros((rows_z - 264, 128), jnp.float32)], axis=0)
        z_ref[c] = z.astype(jnp.bfloat16)
        square = z * z
        high = square.astype(jnp.bfloat16)
        low = (square - high.astype(jnp.float32)).astype(jnp.bfloat16)

        def both(v):
            return jnp.concatenate([v[0:depth], v[offs : offs + depth]], axis=1)

        energy = jnp.dot(band, both(high), preferred_element_type=jnp.float32)
        energy = energy + jnp.dot(band, both(low), preferred_element_type=jnp.float32)
        inv_ref[c] = lax.rsqrt(energy + taps * water_level)

    def windows(first, last, tips):
        def group(i, carry):
            for slot in range(width):
                channel(i * width + slot, tips)
            return carry

        lax.fori_loop(first // width, last // width, group, 0)

    pair_lists(steps, regions, region, order_ref, channels_ref, list_ref)
    load.wait()

    def place(at, row, value):
        ext[at, row : row + value.shape[1]] = value
        turned[at, row : row + value.shape[1]] = pltpu.roll(value, 64, 2)

    def lay_out(i, carry):
        at = pl.ds(pl.multiple_of(i * 16, 16), 16)
        place(at, 0, local[at, :].astype(jnp.float32).reshape(16, blocks, 128))
        return carry

    lax.fori_loop(0, chans // 16, lay_out, 0)
    rest = chans // 16 * 16
    if rest < chans:
        place(pl.ds(rest, chans - rest), 0, local[rest:chans, :].astype(jnp.float32).reshape(chans - rest, blocks, 128))
    for u in range(tiles):
        @pl.when(me != holders[u])
        def _():
            piece(u).wait_send()

    def spread_copy(e):
        peer = sibling if e == 0 else lax.rem(chip + e, chips) * 2 + core
        return pltpu.make_async_remote_copy(
            src_ref=sel, dst_ref=full.at[my_tile], send_sem=two_send.at[e], recv_sem=two_recv.at[my_tile],
            device_id=(peer, region), device_id_type=MESH,
        )

    @pl.when(holding)
    def _():
        for i in range(count):
            @pl.when(me != i)
            def _():
                pltpu.make_async_remote_copy(
                    src_ref=mine.at[0], dst_ref=got.at[i], send_sem=one_send.at[0], recv_sem=one_recv.at[i],
                    device_id=(left, region), device_id_type=MESH,
                ).wait_recv()
        got[me] = mine[my_tile]
        for s in range(steps):
            sel[s] = got[owner_ref[s]]
        full[my_tile] = sel[...]
        for e in range(1, chips):
            spread_copy(e).start()
        spread_copy(0).start()

    @pl.when(me < count - 1)
    def _():
        edge_copy.wait_recv()

    inside = (me < count - 1) & (lax.broadcasted_iota(jnp.int32, (1, depth), 1) < taps - 1)
    rims = []
    for i in range(0, chans, 16):
        end = min(i + 16, chans)
        rim = jnp.where(inside, halo[i:end].astype(jnp.float32), 0.0)
        rims.append(rim[:, 128:])
        place(pl.ds(i, end - i), blocks, rim.reshape(end - i, 2, 128))
    tips = jnp.concatenate(rims + [jnp.zeros((128 - chans, 128), jnp.float32)], axis=0).T
    tips = [tips[0:8], tips[64:72]]
    late = chans * 5 // 6 // width * width
    windows(0, late, tips)

    def pass_copy(v):
        u = 2 * v + core
        return pltpu.make_async_remote_copy(
            src_ref=full.at[u], dst_ref=full.at[u], send_sem=pass_send.at[v], recv_sem=two_recv.at[u],
            device_id=(sibling, region), device_id_type=MESH,
        )

    for v in range(half):
        @pl.when(chip != seats[v])
        def _():
            pass_copy(v).wait_recv()
            pass_copy(v).start()

    windows(late, chans, tips)

    for v in range(half):
        u = 2 * v + 1 - core
        pltpu.make_async_remote_copy(
            src_ref=sel, dst_ref=full.at[u], send_sem=two_send.at[0], recv_sem=two_recv.at[u],
            device_id=(sibling, region), device_id_type=MESH,
        ).wait_recv()

    taps_ref[0 : tiles * steps * 16] = full[...].astype(jnp.float32).reshape(tiles * steps * 16, depth)
    taps_ref[tiles * steps * 16 :] = jnp.zeros((8, depth), jnp.float32)

    @pl.when(me > 0)
    def _():
        edge_copy.wait_send()

    @pl.when(holding)
    def _():
        for e in range(chips):
            spread_copy(e).wait_send()

    for v in range(half):
        @pl.when(chip != seats[v])
        def _():
            pass_copy(v).wait_send()


def pair_kernel(which, first, list_ref, z_ref, inv_ref, taps_ref, out_ref, acc_ref):
    held = out_ref.shape[0]
    tiles = out_ref.shape[2] // 128
    total = list_ref[which, 0, list_ref.shape[2] - 1]
    acc_ref[...] = jnp.zeros_like(acc_ref)

    def shifted(row):
        base = jnp.broadcast_to(taps_ref[pl.ds(row, 1)], (offs, depth))
        return pltpu.roll(base, 0, 1, stride=1, stride_axis=0)

    def entry(e):
        codes = [list_ref[which, 0, 2 * e + i] for i in range(2)]
        matrix = jnp.concatenate([shifted(codes[i] & 1023) for i in range(2)], axis=0).astype(jnp.bfloat16)
        col = (codes[0] >> 10) & 127
        window = jnp.concatenate([z_ref[col, offs * v : offs * v + depth] for v in range(first, first + tiles)], axis=1)
        product = jnp.dot(matrix, window, preferred_element_type=jnp.float32)
        scale = inv_ref[col, :, first * 128 : (first + tiles) * 128]
        return [(codes[i] >> 17, product[i * offs : (i + 1) * offs] * scale) for i in range(2)]

    def group(i, carry):
        done = [entry(i * unroll + u) for u in range(unroll)]
        for both in done:
            for template, value in both:
                acc_ref[template] += value
        return carry

    lax.fori_loop(0, (total + unroll - 1) // unroll, group, 0)
    out_ref[...] = acc_ref[:held].astype(out_ref.dtype)


def finish_kernel(total_time, count, *refs):
    *parts, out_ref, stacked, power_sent, power_got, p_send, p_recv = refs
    me = lax.axis_index("tm")
    region = lax.axis_index("region")
    barrier = pltpu.get_barrier_semaphore()
    for d in range(1, count):
        pl.semaphore_signal(barrier, inc=1, device_id=(lax.rem(me + d, count), region), device_id_type=MESH)
    held = out_ref.shape[0]
    lane = lax.broadcasted_iota(jnp.int32, (1, 128), 1)
    power = jnp.zeros((1, 128), jnp.float32)
    for at in range(held):
        value = parts[-1][at]
        for i in range(0, len(parts) - 1, 2):
            value = value + jnp.concatenate([parts[i][at], parts[i + 1][at]], axis=1).astype(jnp.float32)
        stacked[at] = value
        total = jnp.sum(jnp.sum(value * value, axis=0, keepdims=True), axis=1, keepdims=True)
        power = power + jnp.where(lane == at, total, 0.0)
    power_sent[...] = power
    pl.semaphore_wait(barrier, count - 1)
    copies = []
    for d in range(1, count):
        copy = pltpu.make_async_remote_copy(
            src_ref=power_sent, dst_ref=power_got.at[d - 1], send_sem=p_send.at[d - 1], recv_sem=p_recv.at[d - 1],
            device_id=(lax.rem(me + d, count), region), device_id_type=MESH,
        )
        copy.start()
        copies.append(copy)
    for at in range(held):
        value = stacked[at]
        turned = jnp.concatenate([value[:, :128], value[:, 128:]], axis=0).T
        out_ref[at] = jnp.concatenate([turned[:64], turned[64:]], axis=1)
    for copy in copies:
        copy.wait()
    power = power + jnp.sum(power_got[...], axis=0)
    factor = lax.rsqrt(power / total_time + eps)
    for at in range(held):
        one = jnp.sum(jnp.where(lane == at, factor, 0.0), axis=1, keepdims=True)
        out_ref[at] = out_ref[at] * one


def body(waveform, station_order, library, owner, channels):
    chans, time_local = waveform.shape
    blocks = time_local // 128
    steps, templates, used = channels.shape
    tap_count = library.shape[2]
    count = lax.axis_size("tm")
    regions = lax.axis_size("region")
    per = templates // regions
    held = steps * per
    all_templates = steps * templates
    pairs = all_templates * used
    tiles = templates * used // 16
    lanes = time_local // offs

    vmem = pl.BlockSpec(memory_space=pltpu.VMEM)
    smem = pl.BlockSpec(memory_space=pltpu.SMEM)
    dma = pltpu.SemaphoreType.DMA
    length = -(-(held * used + chans + 2 * unroll + 1) // 128) * 128
    z, inv_scale, taps, lists = pl.pallas_call(
        functools.partial(prepare_kernel, steps, count, regions),
        out_shape=[
            jax.ShapeDtypeStruct((chans, rows_z, 128), jnp.bfloat16),
            jax.ShapeDtypeStruct((chans, offs, lanes), jnp.float32),
            jax.ShapeDtypeStruct((pairs + 8, depth), jnp.float32),
            jax.ShapeDtypeStruct((regions, 1, length), jnp.int32),
        ],
        in_specs=[pl.BlockSpec(memory_space=pltpu.HBM)] * 5,
        out_specs=[vmem] * 4,
        scratch_shapes=[
            pltpu.SMEM((steps,), jnp.int32),
            pltpu.VMEM((templates * used, tap_count), jnp.float32),
            pltpu.VMEM((1, chans), jnp.int32),
            pltpu.VMEM((all_templates, used), jnp.int32),
            dma((4,)),
            pltpu.VMEM((tiles, 16, depth), jnp.bfloat16),
            pltpu.VMEM((count, 16, depth), jnp.bfloat16),
            pltpu.VMEM((steps, 16, depth), jnp.bfloat16),
            pltpu.VMEM((tiles, steps, 16, depth), jnp.bfloat16),
            pltpu.VMEM((chans, depth), jnp.bfloat16),
            pltpu.VMEM((chans, time_local), jnp.bfloat16),
            pltpu.VMEM((chans, blocks + 8, 128), jnp.float32),
            pltpu.VMEM((chans, blocks + 8, 128), jnp.float32),
            dma,
            dma((2,)),
            dma((tiles,)),
            dma((count,)),
            dma((count // 2,)),
            dma((tiles,)),
            dma((tiles // 2,)),
        ],
        compiler_params=pltpu.CompilerParams(collective_id=0, has_side_effects=True, vmem_limit_bytes=28 * 2**20),
        name="prepare",
    )(*[pltpu.with_memory_space_constraint(v, pltpu.HBM) for v in (
        owner, library.reshape(templates * used, tap_count), waveform,
        station_order.reshape(1, chans), channels.reshape(all_templates, used),
    )])

    def partial_sums(which, dtype, first, lanes):
        return pl.pallas_call(
            functools.partial(pair_kernel, which, first),
            out_shape=jax.ShapeDtypeStruct((held, offs, lanes), dtype),
            in_specs=[smem, vmem, vmem, vmem],
            out_specs=vmem,
            scratch_shapes=[pltpu.VMEM((held + 1, offs, lanes), jnp.float32)],
            compiler_params=pltpu.CompilerParams(vmem_limit_bytes=16 * 2**20),
            cost_estimate=pl.CostEstimate(flops=held * used * offs * depth * lanes, bytes_accessed=12 * 2**20, transcendentals=0),
            name="pairs",
        )(lists, z, inv_scale, taps)

    parts = []
    for d in range(1, regions):
        for v in range(lanes // 128):
            part = partial_sums(d - 1, jnp.bfloat16, v, 128)
            parts.append(lax.ppermute(part, "region", [(i, (i + d) % regions) for i in range(regions)]))
    parts.append(partial_sums(regions - 1, jnp.float32, 0, lanes))

    result = pl.pallas_call(
        functools.partial(finish_kernel, time_local * count, count),
        out_shape=jax.ShapeDtypeStruct((held, blocks, 128), jnp.float32),
        in_specs=[vmem] * len(parts),
        out_specs=vmem,
        scratch_shapes=[
            pltpu.VMEM((held, offs, lanes), jnp.float32),
            pltpu.VMEM((1, 128), jnp.float32),
            pltpu.VMEM((count - 1, 1, 128), jnp.float32),
            dma((count - 1,)),
            dma((count - 1,)),
        ],
        compiler_params=pltpu.CompilerParams(collective_id=1, has_side_effects=True, vmem_limit_bytes=16 * 2**20),
        name="finish",
    )(*parts)
    return result.reshape(steps, per, time_local)


def solution(mesh):
    in_specs = (P("region", "tm"), P("region"), P("tm", None, None), P(), P())
    out_specs = P(None, "region", "tm")
    return jax.shard_map(body, mesh=mesh, in_specs=in_specs, out_specs=out_specs, check_vma=False)
```

```python
import functools
import jax
import jax.numpy as jnp
from jax import lax
from jax.experimental import pallas as pl
from jax.experimental.pallas import tpu as pltpu
from jax.sharding import PartitionSpec as P

water_level = 4.0
eps = 1e-06
offs = 32
depth = 256
rows_z = 288
unroll = 64
MESH = pl.DeviceIdType.MESH


def far_first(count):
    return sorted(range(1, count), key=lambda d: abs(d - count // 2))


def pair_lists(steps, regions, region, order_ref, channels_ref, list_ref):
    rows, used = channels_ref.shape
    templates = rows // steps
    per = templates // regions
    held = steps * per
    chans = order_ref.shape[1]
    length = list_ref.shape[2]
    f32, bf16 = jnp.float32, jnp.bfloat16
    order = order_ref[...]
    table = channels_ref[...]
    hit = jnp.zeros((rows, chans), jnp.int32)
    place = jnp.zeros((rows, chans), jnp.int32)
    for j in range(used):
        same = jnp.broadcast_to(table[:, j : j + 1], (rows, chans)) == order
        hit = hit + jnp.where(same, 1, 0)
        place = place + jnp.where(same, j, 0)
    one = lax.broadcasted_iota(jnp.int32, (rows, rows), 0)
    two = lax.broadcasted_iota(jnp.int32, (rows, rows), 1)
    together = one % templates // per == two % templates // per

    def ones(mask):
        return jnp.where(mask, 1.0, 0.0).astype(bf16)

    hits = hit.astype(f32)
    rank = jnp.dot(ones(together & (two < one)), hits.astype(bf16), preferred_element_type=f32)
    amount = jnp.dot(ones(together), hits.astype(bf16), preferred_element_type=f32)
    entries = jnp.floor((amount + 1) * 0.5)
    before = ones(lax.broadcasted_iota(jnp.int32, (chans, chans), 0) < lax.broadcasted_iota(jnp.int32, (chans, chans), 1))
    first = jnp.dot(entries.astype(bf16), before, preferred_element_type=f32)
    position = jnp.where(hits > 0, 2 * first + rank, -1.0)
    row = lax.broadcasted_iota(jnp.int32, (rows, chans), 0)
    step = row // templates
    inner = row % templates * used + place
    source = (inner // 16 * steps + step) * 16 + inner % 16
    target = step * per + row % templates % per
    column = lax.broadcasted_iota(jnp.int32, (rows, chans), 1)
    empty = held * 2**17 + rows * used
    code = (target * 2**17 + column * 2**10 + source - empty).astype(f32)
    blank = jnp.zeros((rows, 128 - chans), f32)
    position = jnp.concatenate([position, blank - 1], axis=1).T
    code = jnp.concatenate([code, blank], axis=1).T
    total = jnp.sum(entries, axis=1, keepdims=True)
    for g in range(regions):
        mine = [s * templates + g * per + k for s in range(steps) for k in range(per)]
        for base in range(0, length, 128):
            index = (lax.broadcasted_iota(jnp.int32, (128, 128), 1) + base).astype(f32)
            found = jnp.zeros((128, 128), f32)
            for t in mine:
                found = found + jnp.where(position[:, t : t + 1] == index, code[:, t : t + 1], 0.0)
            line = jnp.sum(found, axis=0, keepdims=True).astype(jnp.int32) + empty
            if base + 128 == length:
                last = lax.broadcasted_iota(jnp.int32, (1, 128), 1) == 127
                line = jnp.where(last, total[mine[0] : mine[0] + 1].astype(jnp.int32), line)
            list_ref[lax.rem(g - region - 1 + 2 * regions, regions), 0:1, base : base + 128] = line


def prepare_kernel(
    steps, count, regions, owner_hbm, library_hbm, x_ref, order_hbm, channels_hbm, z_ref, inv_ref, taps_ref, list_ref,
    owner_ref, library_ref, order_ref, channels_ref, small_sems, mine, got, sel, full, halo, local, ext, turned, local_sem, halo_sems, one_send, one_recv, two_send, two_recv, pass_send,
):
    me = lax.axis_index("tm")
    region = lax.axis_index("region")
    barrier = pltpu.get_barrier_semaphore()
    for d in far_first(count):
        pl.semaphore_signal(barrier, inc=1, device_id=(lax.rem(me + d, count), region), device_id_type=MESH)
    small = [
        pltpu.make_async_copy(source, target, small_sems.at[i])
        for i, (source, target) in enumerate(
            [(library_hbm, library_ref), (owner_hbm, owner_ref), (order_hbm, order_ref), (channels_hbm, channels_ref)]
        )
    ]
    for copy in small:
        copy.start()
    load = pltpu.make_async_copy(x_ref, local, local_sem)
    load.start()
    small[0].wait()

    taps = library_ref.shape[1]
    units = mine.shape[0]
    seats = full.shape[0]
    share = units // seats
    panel = library_ref[...]
    centred = panel - jnp.sum(panel, axis=1, keepdims=True) * (1 / taps)
    normed = centred * lax.rsqrt(jnp.sum(centred * centred, axis=1, keepdims=True) + eps)
    normed = jnp.concatenate([normed, jnp.zeros((panel.shape[0], depth - taps), jnp.float32)], axis=1)
    normed = normed.astype(jnp.bfloat16)
    for i in range(units):
        mine[i] = normed[i // 2 * 16 : i // 2 * 16 + 16, i % 2 * 128 : i % 2 * 128 + 128]

    first = (count - seats) // 4 * 2
    chips = count // 2
    chip = me // 2
    core = me % 2
    sibling = chip * 2 + 1 - core
    holding = (me >= first) & (me < first + seats)
    seat = jnp.clip(me - first, 0, seats - 1)

    pl.semaphore_wait(barrier, count - 1)
    left = lax.rem(me + count - 1, count)
    edge_copy = pltpu.make_async_remote_copy(
        src_ref=x_ref.at[:, pl.ds(0, depth)], dst_ref=halo, send_sem=halo_sems.at[0], recv_sem=halo_sems.at[1],
        device_id=(left, region), device_id_type=MESH,
    )

    def piece(u):
        return pltpu.make_async_remote_copy(
            src_ref=mine.at[pl.ds(u * share, share)], dst_ref=got.at[me],
            send_sem=one_send.at[u], recv_sem=one_recv.at[me],
            device_id=(first + u, region), device_id_type=MESH,
        )

    for u in range(seats):
        @pl.when(me != first + u)
        def _():
            piece(u).start()

    @pl.when(me > 0)
    def _():
        edge_copy.start()

    chans = x_ref.shape[0]
    blocks = x_ref.shape[1] // 128
    lane = lax.broadcasted_iota(jnp.int32, (1, 128), 1)
    low_half = lane < 64
    spread = lax.broadcasted_iota(jnp.int32, (offs, depth), 1) - lax.broadcasted_iota(jnp.int32, (offs, depth), 0)
    band = ((spread >= 0) & (spread < taps)).astype(jnp.float32).astype(jnp.bfloat16)
    width = 16 if chans % 16 == 0 else 8

    def channel(c, tips):
        y = [turned[c, m : m + blocks] for m in range(3)]
        columns = [
            jnp.concatenate([ext[c, m : m + blocks], jnp.where(low_half, y[m], y[m + 1])], axis=0).T for m in range(2)
        ]
        last = pltpu.roll(columns[0][:8], 126, 1)
        last = jnp.where(lane % 64 == 62, pltpu.roll(columns[1][:8], 127, 1), last)
        last = jnp.where(lane == 63, pltpu.roll(tips[0], lax.rem(191 - c, 128), 1), last)
        last = jnp.where(lane == 127, pltpu.roll(tips[1], 127 - c, 1), last)
        z = jnp.concatenate(columns + [last, jnp.zeros((rows_z - 264, 128), jnp.float32)], axis=0)
        z_ref[c] = z.astype(jnp.bfloat16)
        square = z * z
        high = square.astype(jnp.bfloat16)
        low = (square - high.astype(jnp.float32)).astype(jnp.bfloat16)

        def both(v):
            return jnp.concatenate([v[0:depth], v[offs : offs + depth]], axis=1)

        energy = jnp.dot(band, both(high), preferred_element_type=jnp.float32)
        energy = energy + jnp.dot(band, both(low), preferred_element_type=jnp.float32)
        inv_ref[c] = lax.rsqrt(energy + taps * water_level)

    def windows(first, last, tips):
        def group(i, carry):
            for slot in range(width):
                channel(i * width + slot, tips)
            return carry

        lax.fori_loop(first // width, last // width, group, 0)

    for copy in small[1:]:
        copy.wait()
    pair_lists(steps, regions, region, order_ref, channels_ref, list_ref)
    load.wait()

    def place(at, row, value):
        ext[at, row : row + value.shape[1]] = value
        turned[at, row : row + value.shape[1]] = pltpu.roll(value, 64, 2)

    def lay_out(i, carry):
        at = pl.ds(pl.multiple_of(i * 16, 16), 16)
        place(at, 0, local[at, :].astype(jnp.float32).reshape(16, blocks, 128))
        return carry

    lax.fori_loop(0, chans // 16, lay_out, 0)
    rest = chans // 16 * 16
    if rest < chans:
        place(pl.ds(rest, chans - rest), 0, local[rest:chans, :].astype(jnp.float32).reshape(chans - rest, blocks, 128))
    def spread_copy(e):
        peer = sibling if e == 0 else lax.rem(chip + e, chips) * 2 + core
        return pltpu.make_async_remote_copy(
            src_ref=sel, dst_ref=full.at[seat], send_sem=two_send.at[e], recv_sem=two_recv.at[seat],
            device_id=(peer, region), device_id_type=MESH,
        )

    @pl.when(holding)
    def _():
        for i in range(count):
            @pl.when(me != i)
            def _():
                pltpu.make_async_remote_copy(
                    src_ref=mine.at[pl.ds(0, share)], dst_ref=got.at[i], send_sem=one_send.at[0], recv_sem=one_recv.at[i],
                    device_id=(left, region), device_id_type=MESH,
                ).wait_recv()
        got[me] = mine[pl.ds(seat * share, share)]
        for s in range(steps):
            sel[s] = got[owner_ref[s]]
        full[seat] = sel[...]
        for e in far_first(chips):
            spread_copy(e).start()
        spread_copy(0).start()

    @pl.when(me < count - 1)
    def _():
        edge_copy.wait_recv()

    inside = (me < count - 1) & (lax.broadcasted_iota(jnp.int32, (1, depth), 1) < taps - 1)
    rims = []
    for i in range(0, chans, 16):
        end = min(i + 16, chans)
        rim = jnp.where(inside, halo[i:end].astype(jnp.float32), 0.0)
        rims.append(rim[:, 128:])
        place(pl.ds(i, end - i), blocks, rim.reshape(end - i, 2, 128))
    tips = jnp.concatenate(rims + [jnp.zeros((128 - chans, 128), jnp.float32)], axis=0).T
    tips = [tips[0:8], tips[64:72]]
    late = chans * 5 // 6 // width * width
    windows(0, late, tips)

    def pass_copy(v):
        u = 2 * v + core
        return pltpu.make_async_remote_copy(
            src_ref=full.at[u], dst_ref=full.at[u], send_sem=pass_send.at[v], recv_sem=two_recv.at[u],
            device_id=(sibling, region), device_id_type=MESH,
        )

    for v in range(seats // 2):
        @pl.when(chip != first // 2 + v)
        def _():
            pass_copy(v).wait_recv()
            pass_copy(v).start()

    windows(late, chans, tips)

    for v in range(seats // 2):
        u = 2 * v + 1 - core
        pltpu.make_async_remote_copy(
            src_ref=sel, dst_ref=full.at[u], send_sem=two_send.at[0], recv_sem=two_recv.at[u],
            device_id=(sibling, region), device_id_type=MESH,
        ).wait_recv()

    span = steps * 16
    for i in range(units):
        value = full[i // share, :, i % share].astype(jnp.float32).reshape(span, 128)
        taps_ref[i // 2 * span : i // 2 * span + span, i % 2 * 128 : i % 2 * 128 + 128] = value
    taps_ref[units // 2 * span :] = jnp.zeros((8, depth), jnp.float32)

    @pl.when(me > 0)
    def _():
        edge_copy.wait_send()

    for u in range(seats):
        @pl.when(me != first + u)
        def _():
            piece(u).wait_send()

    @pl.when(holding)
    def _():
        for e in range(chips):
            spread_copy(e).wait_send()

    for v in range(seats // 2):
        @pl.when(chip != first // 2 + v)
        def _():
            pass_copy(v).wait_send()


def pair_kernel(which, first, list_ref, z_ref, inv_ref, taps_ref, out_ref, acc_ref):
    held = out_ref.shape[0]
    tiles = out_ref.shape[2] // 128
    total = list_ref[which, 0, list_ref.shape[2] - 1]
    acc_ref[...] = jnp.zeros_like(acc_ref)

    def shifted(row):
        base = jnp.broadcast_to(taps_ref[pl.ds(row, 1)], (offs, depth))
        return pltpu.roll(base, 0, 1, stride=1, stride_axis=0)

    def entry(e):
        codes = [list_ref[which, 0, 2 * e + i] for i in range(2)]
        matrix = jnp.concatenate([shifted(codes[i] & 1023) for i in range(2)], axis=0).astype(jnp.bfloat16)
        col = (codes[0] >> 10) & 127
        window = jnp.concatenate([z_ref[col, offs * v : offs * v + depth] for v in range(first, first + tiles)], axis=1)
        product = jnp.dot(matrix, window, preferred_element_type=jnp.float32)
        scale = inv_ref[col, :, first * 128 : (first + tiles) * 128]
        return [(codes[i] >> 17, product[i * offs : (i + 1) * offs] * scale) for i in range(2)]

    def group(i, carry):
        done = [entry(i * unroll + u) for u in range(unroll)]
        for both in done:
            for template, value in both:
                acc_ref[template] += value
        return carry

    lax.fori_loop(0, (total + unroll - 1) // unroll, group, 0)
    out_ref[...] = acc_ref[:held].astype(out_ref.dtype)


def finish_kernel(total_time, count, *refs):
    *parts, out_ref, stacked, power_sent, power_got, p_send, p_recv = refs
    me = lax.axis_index("tm")
    region = lax.axis_index("region")
    barrier = pltpu.get_barrier_semaphore()
    for d in far_first(count):
        pl.semaphore_signal(barrier, inc=1, device_id=(lax.rem(me + d, count), region), device_id_type=MESH)
    held = out_ref.shape[0]
    squares = []
    for at in range(held):
        value = parts[-1][at]
        for i in range(0, len(parts) - 1, 2):
            value = value + jnp.concatenate([parts[i][at], parts[i + 1][at]], axis=1).astype(jnp.float32)
        stacked[at] = value
        square = value * value
        square = square[:, :128] + square[:, 128:]
        squares.append(jnp.sum(square.reshape(offs // 8, 8, 128), axis=0)[None])
    power = jnp.sum(jnp.sum(jnp.concatenate(squares, axis=0), axis=1), axis=1, keepdims=True)
    diagonal = lax.broadcasted_iota(jnp.int32, (held, 128), 0) == lax.broadcasted_iota(jnp.int32, (held, 128), 1)
    power = jnp.sum(jnp.where(diagonal, power, 0.0), axis=0, keepdims=True)
    power_sent[...] = power
    pl.semaphore_wait(barrier, count - 1)
    copies = []
    for d in far_first(count):
        copy = pltpu.make_async_remote_copy(
            src_ref=power_sent, dst_ref=power_got.at[d - 1], send_sem=p_send.at[d - 1], recv_sem=p_recv.at[d - 1],
            device_id=(lax.rem(me + d, count), region), device_id_type=MESH,
        )
        copy.start()
        copies.append(copy)
    for at in range(held):
        value = stacked[at]
        turned = jnp.concatenate([value[:, :128], value[:, 128:]], axis=0).T
        out_ref[at] = jnp.concatenate([turned[:64], turned[64:]], axis=1)
    for copy in copies:
        copy.wait_recv()
    power = power + jnp.sum(power_got[...], axis=0)
    factor = lax.rsqrt(power / total_time + eps)
    scale = jnp.sum(jnp.where(diagonal, factor, 0.0), axis=1, keepdims=True)
    for at in range(held):
        out_ref[at] = out_ref[at] * scale[at : at + 1]
    for copy in copies:
        copy.wait_send()


def body(waveform, station_order, library, owner, channels):
    chans, time_local = waveform.shape
    blocks = time_local // 128
    steps, templates, used = channels.shape
    tap_count = library.shape[2]
    count = lax.axis_size("tm")
    regions = lax.axis_size("region")
    per = templates // regions
    held = steps * per
    all_templates = steps * templates
    pairs = all_templates * used
    units = templates * used // 8
    seats = 8
    lanes = time_local // offs

    vmem = pl.BlockSpec(memory_space=pltpu.VMEM)
    smem = pl.BlockSpec(memory_space=pltpu.SMEM)
    dma = pltpu.SemaphoreType.DMA
    length = -(-(held * used + chans + 2 * unroll + 1) // 128) * 128
    z, inv_scale, taps, lists = pl.pallas_call(
        functools.partial(prepare_kernel, steps, count, regions),
        out_shape=[
            jax.ShapeDtypeStruct((chans, rows_z, 128), jnp.bfloat16),
            jax.ShapeDtypeStruct((chans, offs, lanes), jnp.float32),
            jax.ShapeDtypeStruct((pairs + 8, depth), jnp.float32),
            jax.ShapeDtypeStruct((regions, 1, length), jnp.int32),
        ],
        in_specs=[pl.BlockSpec(memory_space=pltpu.HBM)] * 5,
        out_specs=[vmem] * 4,
        scratch_shapes=[
            pltpu.SMEM((steps,), jnp.int32),
            pltpu.VMEM((templates * used, tap_count), jnp.float32),
            pltpu.VMEM((1, chans), jnp.int32),
            pltpu.VMEM((all_templates, used), jnp.int32),
            dma((4,)),
            pltpu.VMEM((units, 16, 128), jnp.bfloat16),
            pltpu.VMEM((count, units // seats, 16, 128), jnp.bfloat16),
            pltpu.VMEM((steps, units // seats, 16, 128), jnp.bfloat16),
            pltpu.VMEM((seats, steps, units // seats, 16, 128), jnp.bfloat16),
            pltpu.VMEM((chans, depth), jnp.bfloat16),
            pltpu.VMEM((chans, time_local), jnp.bfloat16),
            pltpu.VMEM((chans, blocks + 8, 128), jnp.float32),
            pltpu.VMEM((chans, blocks + 8, 128), jnp.float32),
            dma,
            dma((2,)),
            dma((seats,)),
            dma((count,)),
            dma((count // 2,)),
            dma((seats,)),
            dma((seats // 2,)),
        ],
        compiler_params=pltpu.CompilerParams(collective_id=0, has_side_effects=True, vmem_limit_bytes=28 * 2**20),
        name="prepare",
    )(*[pltpu.with_memory_space_constraint(v, pltpu.HBM) for v in (
        owner, library.reshape(templates * used, tap_count), waveform,
        station_order.reshape(1, chans), channels.reshape(all_templates, used),
    )])

    def partial_sums(which, dtype, first, lanes):
        return pl.pallas_call(
            functools.partial(pair_kernel, which, first),
            out_shape=jax.ShapeDtypeStruct((held, offs, lanes), dtype),
            in_specs=[smem, vmem, vmem, vmem],
            out_specs=vmem,
            scratch_shapes=[pltpu.VMEM((held + 1, offs, lanes), jnp.float32)],
            compiler_params=pltpu.CompilerParams(vmem_limit_bytes=16 * 2**20),
            cost_estimate=pl.CostEstimate(flops=held * used * offs * depth * lanes, bytes_accessed=12 * 2**20, transcendentals=0),
            name="pairs",
        )(lists, z, inv_scale, taps)

    parts = []
    for d in range(1, regions):
        for v in range(lanes // 128):
            part = partial_sums(d - 1, jnp.bfloat16, v, 128)
            parts.append(lax.ppermute(part, "region", [(i, (i + d) % regions) for i in range(regions)]))
    parts.append(partial_sums(regions - 1, jnp.float32, 0, lanes))

    result = pl.pallas_call(
        functools.partial(finish_kernel, time_local * count, count),
        out_shape=jax.ShapeDtypeStruct((held, blocks, 128), jnp.float32),
        in_specs=[vmem] * len(parts),
        out_specs=vmem,
        scratch_shapes=[
            pltpu.VMEM((held, offs, lanes), jnp.float32),
            pltpu.VMEM((1, 128), jnp.float32),
            pltpu.VMEM((count - 1, 1, 128), jnp.float32),
            dma((count - 1,)),
            dma((count - 1,)),
        ],
        compiler_params=pltpu.CompilerParams(collective_id=1, has_side_effects=True, vmem_limit_bytes=16 * 2**20),
        name="finish",
    )(*parts)
    return result.reshape(steps, per, time_local)


def solution(mesh):
    in_specs = (P("region", "tm"), P("region"), P("tm", None, None), P(), P())
    out_specs = P(None, "region", "tm")
    return jax.shard_map(body, mesh=mesh, in_specs=in_specs, out_specs=out_specs, check_vma=False)
```

```python
import functools
import jax
import jax.numpy as jnp
from jax import lax
from jax.experimental import pallas as pl
from jax.experimental.pallas import tpu as pltpu
from jax.sharding import PartitionSpec as P

water_level = 4.0
eps = 1e-06
offs = 32
depth = 256
rows_z = 288
unroll = 64
few = 16
MESH = pl.DeviceIdType.MESH


def far_first(count):
    return sorted(range(1, count), key=lambda d: abs(d - count // 2))


def pair_lists(steps, regions, region, order_ref, channels_ref, list_ref):
    rows, used = channels_ref.shape
    templates = rows // steps
    per = templates // regions
    held = steps * per
    chans = order_ref.shape[1]
    length = list_ref.shape[2]
    f32, bf16 = jnp.float32, jnp.bfloat16
    order = order_ref[...]
    table = channels_ref[...]
    hit = jnp.zeros((rows, chans), jnp.int32)
    place = jnp.zeros((rows, chans), jnp.int32)
    for j in range(used):
        same = jnp.broadcast_to(table[:, j : j + 1], (rows, chans)) == order
        hit = hit + jnp.where(same, 1, 0)
        place = place + jnp.where(same, j, 0)
    one = lax.broadcasted_iota(jnp.int32, (rows, rows), 0)
    two = lax.broadcasted_iota(jnp.int32, (rows, rows), 1)
    together = one % templates // per == two % templates // per

    def ones(mask):
        return jnp.where(mask, 1.0, 0.0).astype(bf16)

    hits = hit.astype(f32)
    rank = jnp.dot(ones(together & (two < one)), hits.astype(bf16), preferred_element_type=f32)
    amount = jnp.dot(ones(together), hits.astype(bf16), preferred_element_type=f32)
    entries = jnp.floor((amount + 1) * 0.5)
    before = ones(lax.broadcasted_iota(jnp.int32, (chans, chans), 0) < lax.broadcasted_iota(jnp.int32, (chans, chans), 1))
    first = jnp.dot(entries.astype(bf16), before, preferred_element_type=f32)
    position = jnp.where(hits > 0, 2 * first + rank, -1.0)
    row = lax.broadcasted_iota(jnp.int32, (rows, chans), 0)
    step = row // templates
    inner = row % templates * used + place
    source = (inner // 16 * steps + step) * 16 + inner % 16
    target = step * per + row % templates % per
    column = lax.broadcasted_iota(jnp.int32, (rows, chans), 1)
    empty = held * 2**17 + rows * used
    code = (target * 2**17 + column * 2**10 + source - empty).astype(f32)
    blank = jnp.zeros((rows, 128 - chans), f32)
    position = jnp.concatenate([position, blank - 1], axis=1).T
    code = jnp.concatenate([code, blank], axis=1).T
    total = jnp.sum(entries, axis=1, keepdims=True)
    for g in range(regions):
        mine = [s * templates + g * per + k for s in range(steps) for k in range(per)]
        for base in range(0, length, 128):
            index = (lax.broadcasted_iota(jnp.int32, (128, 128), 1) + base).astype(f32)
            found = jnp.zeros((128, 128), f32)
            for t in mine:
                found = found + jnp.where(position[:, t : t + 1] == index, code[:, t : t + 1], 0.0)
            line = jnp.sum(found, axis=0, keepdims=True).astype(jnp.int32) + empty
            if base + 128 == length:
                last = lax.broadcasted_iota(jnp.int32, (1, 128), 1) == 127
                line = jnp.where(last, total[mine[0] : mine[0] + 1].astype(jnp.int32), line)
            list_ref[lax.rem(g - region - 1 + 2 * regions, regions), 0:1, base : base + 128] = line


def prepare_kernel(
    steps, count, regions, owner_hbm, library_hbm, x_ref, order_hbm, channels_hbm, z_ref, inv_ref, taps_ref, list_ref,
    owner_ref, library_ref, order_ref, channels_ref, small_sems, mine, got, sel, full, halo, local, ext, turned, local_sem, halo_sems, one_send, one_recv, two_send, two_recv, pass_send,
):
    me = lax.axis_index("tm")
    region = lax.axis_index("region")
    barrier = pltpu.get_barrier_semaphore()
    for d in far_first(count):
        pl.semaphore_signal(barrier, inc=1, device_id=(lax.rem(me + d, count), region), device_id_type=MESH)
    small = [
        pltpu.make_async_copy(source, target, small_sems.at[i])
        for i, (source, target) in enumerate(
            [(library_hbm, library_ref), (owner_hbm, owner_ref), (order_hbm, order_ref), (channels_hbm, channels_ref)]
        )
    ]
    for copy in small:
        copy.start()
    load = pltpu.make_async_copy(x_ref, local, local_sem)
    load.start()
    small[0].wait()

    taps = library_ref.shape[1]
    units = mine.shape[0]
    seats = full.shape[0]
    share = units // seats
    panel = library_ref[...]
    centred = panel - jnp.sum(panel, axis=1, keepdims=True) * (1 / taps)
    normed = centred * lax.rsqrt(jnp.sum(centred * centred, axis=1, keepdims=True) + eps)
    normed = jnp.concatenate([normed, jnp.zeros((panel.shape[0], depth - taps), jnp.float32)], axis=1)
    normed = normed.astype(jnp.bfloat16)
    for i in range(units):
        mine[i] = normed[i // 2 * 16 : i // 2 * 16 + 16, i % 2 * 128 : i % 2 * 128 + 128]

    first = (count - seats) // 4 * 2
    chips = count // 2
    chip = me // 2
    core = me % 2
    sibling = chip * 2 + 1 - core
    holding = (me >= first) & (me < first + seats)
    seat = jnp.clip(me - first, 0, seats - 1)

    pl.semaphore_wait(barrier, count - 1)
    left = lax.rem(me + count - 1, count)
    edge_copy = pltpu.make_async_remote_copy(
        src_ref=x_ref.at[:, pl.ds(0, depth)], dst_ref=halo, send_sem=halo_sems.at[0], recv_sem=halo_sems.at[1],
        device_id=(left, region), device_id_type=MESH,
    )

    def piece(u):
        return pltpu.make_async_remote_copy(
            src_ref=mine.at[pl.ds(u * share, share)], dst_ref=got.at[me],
            send_sem=one_send.at[u], recv_sem=one_recv.at[me],
            device_id=(first + u, region), device_id_type=MESH,
        )

    for u in range(seats):
        @pl.when(me != first + u)
        def _():
            piece(u).start()

    @pl.when(me > 0)
    def _():
        edge_copy.start()

    chans = x_ref.shape[0]
    blocks = x_ref.shape[1] // 128
    lane = lax.broadcasted_iota(jnp.int32, (1, 128), 1)
    low_half = lane < 64
    spread = lax.broadcasted_iota(jnp.int32, (offs, depth), 1) - lax.broadcasted_iota(jnp.int32, (offs, depth), 0)
    band = ((spread >= 0) & (spread < taps)).astype(jnp.float32).astype(jnp.bfloat16)
    width = 16 if chans % 16 == 0 else 8

    def channel(c, tips):
        y = [turned[c, m : m + blocks] for m in range(3)]
        columns = [
            jnp.concatenate([ext[c, m : m + blocks], jnp.where(low_half, y[m], y[m + 1])], axis=0).T for m in range(2)
        ]
        last = pltpu.roll(columns[0][:8], 126, 1)
        last = jnp.where(lane % 64 == 62, pltpu.roll(columns[1][:8], 127, 1), last)
        last = jnp.where(lane == 63, pltpu.roll(tips[0], lax.rem(191 - c, 128), 1), last)
        last = jnp.where(lane == 127, pltpu.roll(tips[1], 127 - c, 1), last)
        z = jnp.concatenate(columns + [last, jnp.zeros((rows_z - 264, 128), jnp.float32)], axis=0)
        z_ref[c] = z.astype(jnp.bfloat16)
        square = z * z
        high = square.astype(jnp.bfloat16)
        low = (square - high.astype(jnp.float32)).astype(jnp.bfloat16)

        def both(v):
            return jnp.concatenate([v[0:depth], v[offs : offs + depth]], axis=1)

        energy = jnp.dot(band, both(high), preferred_element_type=jnp.float32)
        energy = energy + jnp.dot(band, both(low), preferred_element_type=jnp.float32)
        inv_ref[c] = lax.rsqrt(energy + taps * water_level)

    def windows(first, last, tips):
        def group(i, carry):
            for slot in range(width):
                channel(i * width + slot, tips)
            return carry

        lax.fori_loop(first // width, last // width, group, 0)

    for copy in small[1:]:
        copy.wait()
    pair_lists(steps, regions, region, order_ref, channels_ref, list_ref)
    load.wait()

    def place(at, row, value):
        ext[at, row : row + value.shape[1]] = value
        turned[at, row : row + value.shape[1]] = pltpu.roll(value, 64, 2)

    def lay_out(i, carry):
        at = pl.ds(pl.multiple_of(i * 16, 16), 16)
        place(at, 0, local[at, :].astype(jnp.float32).reshape(16, blocks, 128))
        return carry

    lax.fori_loop(0, chans // 16, lay_out, 0)
    rest = chans // 16 * 16
    if rest < chans:
        place(pl.ds(rest, chans - rest), 0, local[rest:chans, :].astype(jnp.float32).reshape(chans - rest, blocks, 128))
    def spread_copy(e):
        peer = sibling if e == 0 else lax.rem(chip + e, chips) * 2 + core
        return pltpu.make_async_remote_copy(
            src_ref=sel, dst_ref=full.at[seat], send_sem=two_send.at[e], recv_sem=two_recv.at[seat],
            device_id=(peer, region), device_id_type=MESH,
        )

    @pl.when(holding)
    def _():
        for i in range(count):
            @pl.when(me != i)
            def _():
                pltpu.make_async_remote_copy(
                    src_ref=mine.at[pl.ds(0, share)], dst_ref=got.at[i], send_sem=one_send.at[0], recv_sem=one_recv.at[i],
                    device_id=(left, region), device_id_type=MESH,
                ).wait_recv()
        got[me] = mine[pl.ds(seat * share, share)]
        for s in range(steps):
            sel[s] = got[owner_ref[s]]
        full[seat] = sel[...]
        for e in far_first(chips):
            spread_copy(e).start()
        spread_copy(0).start()

    @pl.when(me < count - 1)
    def _():
        edge_copy.wait_recv()

    inside = (me < count - 1) & (lax.broadcasted_iota(jnp.int32, (1, depth), 1) < taps - 1)
    rims = []
    for i in range(0, chans, 16):
        end = min(i + 16, chans)
        rim = jnp.where(inside, halo[i:end].astype(jnp.float32), 0.0)
        rims.append(rim[:, 128:])
        place(pl.ds(i, end - i), blocks, rim.reshape(end - i, 2, 128))
    tips = jnp.concatenate(rims + [jnp.zeros((128 - chans, 128), jnp.float32)], axis=0).T
    tips = [tips[0:8], tips[64:72]]
    late = chans * 5 // 6 // width * width
    windows(0, late, tips)

    def pass_copy(v):
        u = 2 * v + core
        return pltpu.make_async_remote_copy(
            src_ref=full.at[u], dst_ref=full.at[u], send_sem=pass_send.at[v], recv_sem=two_recv.at[u],
            device_id=(sibling, region), device_id_type=MESH,
        )

    for v in range(seats // 2):
        @pl.when(chip != first // 2 + v)
        def _():
            pass_copy(v).wait_recv()
            pass_copy(v).start()

    windows(late, chans, tips)

    for v in range(seats // 2):
        u = 2 * v + 1 - core
        pltpu.make_async_remote_copy(
            src_ref=sel, dst_ref=full.at[u], send_sem=two_send.at[0], recv_sem=two_recv.at[u],
            device_id=(sibling, region), device_id_type=MESH,
        ).wait_recv()

    span = steps * 16
    for i in range(units):
        value = full[i // share, :, i % share].astype(jnp.float32).reshape(span, 128)
        taps_ref[i // 2 * span : i // 2 * span + span, i % 2 * 128 : i % 2 * 128 + 128] = value
    taps_ref[units // 2 * span :] = jnp.zeros((8, depth), jnp.float32)

    @pl.when(me > 0)
    def _():
        edge_copy.wait_send()

    for u in range(seats):
        @pl.when(me != first + u)
        def _():
            piece(u).wait_send()

    @pl.when(holding)
    def _():
        for e in range(chips):
            spread_copy(e).wait_send()

    for v in range(seats // 2):
        @pl.when(chip != first // 2 + v)
        def _():
            pass_copy(v).wait_send()


def pair_kernel(which, first, list_ref, z_ref, inv_ref, taps_ref, out_ref, acc_ref):
    held = out_ref.shape[0]
    tiles = out_ref.shape[2] // 128
    total = list_ref[which, 0, list_ref.shape[2] - 1]
    acc_ref[...] = jnp.zeros_like(acc_ref)

    def shifted(row):
        base = jnp.broadcast_to(taps_ref[pl.ds(row, 1)], (offs, depth))
        return pltpu.roll(base, 0, 1, stride=1, stride_axis=0)

    def entry(e):
        codes = [list_ref[which, 0, 2 * e + i] for i in range(2)]
        matrix = jnp.concatenate([shifted(codes[i] & 1023) for i in range(2)], axis=0).astype(jnp.bfloat16)
        col = (codes[0] >> 10) & 127
        window = jnp.concatenate([z_ref[col, offs * v : offs * v + depth] for v in range(first, first + tiles)], axis=1)
        product = jnp.dot(matrix, window, preferred_element_type=jnp.float32)
        scale = inv_ref[col, :, first * 128 : (first + tiles) * 128]
        return [(codes[i] >> 17, product[i * offs : (i + 1) * offs] * scale) for i in range(2)]

    def entries(start, size):
        done = [entry(start + u) for u in range(size)]
        for both in done:
            for template, value in both:
                acc_ref[template] += value

    def group(i, carry):
        entries(i * unroll, unroll)
        return carry

    def small_group(i, carry):
        entries(groups * unroll + i * few, few)
        return carry

    groups = (total + unroll - few - 1) // unroll
    lax.fori_loop(0, groups, group, 0)
    rest = jnp.maximum(total - groups * unroll, 0)
    lax.fori_loop(0, (rest + few - 1) // few, small_group, 0)
    out_ref[...] = acc_ref[:held].astype(out_ref.dtype)


def finish_kernel(total_time, count, *refs):
    *parts, out_ref, stacked, power_sent, power_got, p_send, p_recv = refs
    me = lax.axis_index("tm")
    region = lax.axis_index("region")
    barrier = pltpu.get_barrier_semaphore()
    for d in far_first(count):
        pl.semaphore_signal(barrier, inc=1, device_id=(lax.rem(me + d, count), region), device_id_type=MESH)
    held = out_ref.shape[0]
    squares = []
    for at in range(held):
        value = parts[-1][at]
        for i in range(0, len(parts) - 1, 2):
            value = value + jnp.concatenate([parts[i][at], parts[i + 1][at]], axis=1).astype(jnp.float32)
        stacked[at] = value
        square = value * value
        square = square[:, :128] + square[:, 128:]
        squares.append(jnp.sum(square.reshape(offs // 8, 8, 128), axis=0)[None])
    power = jnp.sum(jnp.sum(jnp.concatenate(squares, axis=0), axis=1), axis=1, keepdims=True)
    diagonal = lax.broadcasted_iota(jnp.int32, (held, 128), 0) == lax.broadcasted_iota(jnp.int32, (held, 128), 1)
    power = jnp.sum(jnp.where(diagonal, power, 0.0), axis=0, keepdims=True)
    power_sent[...] = power
    pl.semaphore_wait(barrier, count - 1)
    copies = []
    for d in far_first(count):
        copy = pltpu.make_async_remote_copy(
            src_ref=power_sent, dst_ref=power_got.at[d - 1], send_sem=p_send.at[d - 1], recv_sem=p_recv.at[d - 1],
            device_id=(lax.rem(me + d, count), region), device_id_type=MESH,
        )
        copy.start()
        copies.append(copy)
    for at in range(held):
        value = stacked[at]
        turned = jnp.concatenate([value[:, :128], value[:, 128:]], axis=0).T
        out_ref[at] = jnp.concatenate([turned[:64], turned[64:]], axis=1)
    for copy in copies:
        copy.wait_recv()
    power = power + jnp.sum(power_got[...], axis=0)
    factor = lax.rsqrt(power / total_time + eps)
    scale = jnp.sum(jnp.where(diagonal, factor, 0.0), axis=1, keepdims=True)
    for at in range(held):
        out_ref[at] = out_ref[at] * scale[at : at + 1]
    for copy in copies:
        copy.wait_send()


def body(waveform, station_order, library, owner, channels):
    chans, time_local = waveform.shape
    blocks = time_local // 128
    steps, templates, used = channels.shape
    tap_count = library.shape[2]
    count = lax.axis_size("tm")
    regions = lax.axis_size("region")
    per = templates // regions
    held = steps * per
    all_templates = steps * templates
    pairs = all_templates * used
    units = templates * used // 8
    seats = 8
    lanes = time_local // offs

    vmem = pl.BlockSpec(memory_space=pltpu.VMEM)
    smem = pl.BlockSpec(memory_space=pltpu.SMEM)
    dma = pltpu.SemaphoreType.DMA
    length = -(-(held * used + chans + 2 * unroll + 1) // 128) * 128
    z, inv_scale, taps, lists = pl.pallas_call(
        functools.partial(prepare_kernel, steps, count, regions),
        out_shape=[
            jax.ShapeDtypeStruct((chans, rows_z, 128), jnp.bfloat16),
            jax.ShapeDtypeStruct((chans, offs, lanes), jnp.float32),
            jax.ShapeDtypeStruct((pairs + 8, depth), jnp.float32),
            jax.ShapeDtypeStruct((regions, 1, length), jnp.int32),
        ],
        in_specs=[pl.BlockSpec(memory_space=pltpu.HBM)] * 5,
        out_specs=[vmem] * 4,
        scratch_shapes=[
            pltpu.SMEM((steps,), jnp.int32),
            pltpu.VMEM((templates * used, tap_count), jnp.float32),
            pltpu.VMEM((1, chans), jnp.int32),
            pltpu.VMEM((all_templates, used), jnp.int32),
            dma((4,)),
            pltpu.VMEM((units, 16, 128), jnp.bfloat16),
            pltpu.VMEM((count, units // seats, 16, 128), jnp.bfloat16),
            pltpu.VMEM((steps, units // seats, 16, 128), jnp.bfloat16),
            pltpu.VMEM((seats, steps, units // seats, 16, 128), jnp.bfloat16),
            pltpu.VMEM((chans, depth), jnp.bfloat16),
            pltpu.VMEM((chans, time_local), jnp.bfloat16),
            pltpu.VMEM((chans, blocks + 8, 128), jnp.float32),
            pltpu.VMEM((chans, blocks + 8, 128), jnp.float32),
            dma,
            dma((2,)),
            dma((seats,)),
            dma((count,)),
            dma((count // 2,)),
            dma((seats,)),
            dma((seats // 2,)),
        ],
        compiler_params=pltpu.CompilerParams(collective_id=0, has_side_effects=True, vmem_limit_bytes=28 * 2**20),
        name="prepare",
    )(*[pltpu.with_memory_space_constraint(v, pltpu.HBM) for v in (
        owner, library.reshape(templates * used, tap_count), waveform,
        station_order.reshape(1, chans), channels.reshape(all_templates, used),
    )])

    def partial_sums(which, dtype, first, lanes):
        return pl.pallas_call(
            functools.partial(pair_kernel, which, first),
            out_shape=jax.ShapeDtypeStruct((held, offs, lanes), dtype),
            in_specs=[smem, vmem, vmem, vmem],
            out_specs=vmem,
            scratch_shapes=[pltpu.VMEM((held + 1, offs, lanes), jnp.float32)],
            compiler_params=pltpu.CompilerParams(vmem_limit_bytes=16 * 2**20),
            cost_estimate=pl.CostEstimate(flops=held * used * offs * depth * lanes, bytes_accessed=12 * 2**20, transcendentals=0),
            name="pairs",
        )(lists, z, inv_scale, taps)

    parts = []
    for d in range(1, regions):
        for v in range(lanes // 128):
            part = partial_sums(d - 1, jnp.bfloat16, v, 128)
            parts.append(lax.ppermute(part, "region", [(i, (i + d) % regions) for i in range(regions)]))
    parts.append(partial_sums(regions - 1, jnp.float32, 0, lanes))

    result = pl.pallas_call(
        functools.partial(finish_kernel, time_local * count, count),
        out_shape=jax.ShapeDtypeStruct((held, blocks, 128), jnp.float32),
        in_specs=[vmem] * len(parts),
        out_specs=vmem,
        scratch_shapes=[
            pltpu.VMEM((held, offs, lanes), jnp.float32),
            pltpu.VMEM((1, 128), jnp.float32),
            pltpu.VMEM((count - 1, 1, 128), jnp.float32),
            dma((count - 1,)),
            dma((count - 1,)),
        ],
        compiler_params=pltpu.CompilerParams(collective_id=1, has_side_effects=True, vmem_limit_bytes=16 * 2**20),
        name="finish",
    )(*parts)
    return result.reshape(steps, per, time_local)


def solution(mesh):
    in_specs = (P("region", "tm"), P("region"), P("tm", None, None), P(), P())
    out_specs = P(None, "region", "tm")
    return jax.shard_map(body, mesh=mesh, in_specs=in_specs, out_specs=out_specs, check_vma=False)
```
